512 devices in a mesh: grp: 16 (over x, z_hi), body: 32 (over y, z_lo, core).
Axes of the slice: x: 4, y: 8, z: 8 (z_hi: 4, z_lo: 2; z = z_hi * 2 + z_lo), core: 2. Of those that a mesh axis runs over, the one named last changes fastest.
Arguments:
- incident: bfloat16 [512, 16, 512], P(('grp', 'body')), may hold values from -6 to 6
- exciting: float32 [512, 16, 512], P(('grp', 'body')), may hold values from -6 to 6
- t_matrices: bfloat16 [512, 2, 256, 256], P(('grp', 'body')), may hold values from -0.1875 to 0.1875
- hankel_rows: bfloat16 [225, 2, 512], replicated, may hold values from -0.046875 to 0.046875
- offsets: int32 [512, 32], P(('grp', 'body')), may hold values from 0 to 224
- lattice_slots: int32 [512], P('grp'), may hold values from 0 to 31, as said below
- up_maps: bfloat16 [512, 2, 256, 512], P(('grp', 'body')), may hold values from -0.0625 to 0.0625
- down_maps: bfloat16 [512, 2, 512, 256], P(('grp', 'body')), may hold values from -0.1875 to 0.1875
- group_maps: bfloat16 [16, 16, 2, 512, 512], P('grp', None, None, 'body'), may hold values from -0.046875 to 0.046875
Outputs:
- updated: float32 [512, 16, 512], P(('grp', 'body'))
The draws below stay inside these ranges and needn't reach their ends.
Inputs may be any that keep to these rules, and one draw needn't show every extreme that they name: `lattice_slots`: within each group the 32 columns stand at the slots 0 to 31, one column a slot.
All inputs are finite; a program needn't handle non-finite values.
Results may differ from the reference program's by a relative error of at most 0.0034.
Values may be sent and summed in bfloat16 or wider, within the bound.
A program may use at most 64 MiB of HBM per device.

```python
import jax
import jax.numpy as jnp
from jax import lax

P_SIZE = 256
Q = 512
L = 16
NTAB = 225
G = 16
GB = 32
NB = 512


def draw_lattice_slots(key, part):
    group_keys = jax.random.split(jax.random.fold_in(key, 11), G)
    orders = jax.vmap(lambda group_key: jax.random.permutation(group_key, GB))(group_keys)
    return orders.reshape(-1).astype(jnp.int32)


def set_ends(values, key, smallest, high):
    extent = values.shape
    spot = [jax.random.randint(jax.random.fold_in(key, axis), (), 0, extent[axis]) for axis in range(len(extent))]
    values = values.at[tuple(spot)].set(smallest)
    longest = extent.index(max(extent))
    spot[longest] = (spot[longest] + 1) % extent[longest]
    return values.at[tuple(spot)].set(high)


def block_scale(own_key, dims, pieces, smallest, largest):
    loudness = 1.0
    for dim, parts in pieces:
        heights = jax.random.uniform(jax.random.fold_in(jax.random.fold_in(own_key, 6), dim), (parts,), jnp.float32, smallest / len(pieces), largest / len(pieces))
        loudness = loudness * jnp.repeat(jnp.exp(heights), dims[dim] // parts).reshape((-1,) + (1,) * (len(dims) - 1 - dim))
    return loudness


def normal_values(key, shape, width, bound, shards=(), kind=jnp.bfloat16):
    drawn = jax.random.normal(key, shape, jnp.float32) * width
    if len(shards) > 0:
        drawn = block_scale(key, shape, shards, -0.22, 0.18) * drawn
    return jnp.clip(drawn, min=-bound, max=bound).astype(kind)


def setup_inputs(seed: int = 0) -> dict:
    splits = jax.random.split(jax.random.key(seed), 10)
    incident = normal_values(splits[0], (NB, L, 2 * P_SIZE), 1.0, 6.0, ((0, 512),))
    exciting = normal_values(splits[1], (NB, L, 2 * P_SIZE), 1.0, 6.0, ((0, 512),), jnp.float32)
    t_matrices = normal_values(splits[2], (NB, 2, P_SIZE, P_SIZE), (4 * P_SIZE) ** -0.5, 0.1875, ((0, 512),))
    hankel_rows = normal_values(splits[3], (NTAB, 2, 2 * P_SIZE), (2 * P_SIZE * GB) ** -0.5, 0.046875)
    offsets = set_ends(jax.random.randint(splits[4], (NB, GB), 0, NTAB), jax.random.fold_in(splits[4], 1), 0, NTAB - 1).astype(jnp.int32)
    lattice_slots = draw_lattice_slots(jax.random.fold_in(splits[9], 71), 0)
    up_maps = normal_values(splits[6], (NB, 2, P_SIZE, Q), (P_SIZE * GB) ** -0.5, 0.0625, ((0, 512),))
    down_maps = normal_values(splits[7], (NB, 2, Q, P_SIZE), (2 * Q) ** -0.5, 0.1875, ((0, 512),))
    group_maps = normal_values(splits[8], (G, G, 2, Q, Q), (2 * Q * G) ** -0.5, 0.046875, ((0, 16), (3, 32)))
    return dict(incident=incident, exciting=exciting, t_matrices=t_matrices, hankel_rows=hankel_rows, offsets=offsets, lattice_slots=lattice_slots, up_maps=up_maps, down_maps=down_maps, group_maps=group_maps)


def complex_apply(form, values, real_mats, imag_mats):
    half_width = values.shape[-1] // 2
    real_values = values[..., :half_width].astype(jnp.float32)
    imag_values = values[..., half_width:].astype(jnp.float32)
    real_mats = real_mats.astype(jnp.float32)
    imag_mats = imag_mats.astype(jnp.float32)
    real_out = jnp.einsum(form, real_values, real_mats) - jnp.einsum(form, imag_values, imag_mats)
    imag_out = jnp.einsum(form, real_values, imag_mats) + jnp.einsum(form, imag_values, real_mats)
    return jnp.concatenate([real_out, imag_out], axis=-1)


def toeplitz_mats(sequences):
    length = sequences.shape[-1] // 2
    row_index = jnp.arange(length, dtype=jnp.int32)[:, None]
    col_index = jnp.arange(length, dtype=jnp.int32)[None, :]
    return sequences[..., length + col_index - row_index]


def reference(incident, exciting, t_matrices, hankel_rows, offsets, lattice_slots, up_maps, down_maps, group_maps):
    def scatter_one(inputs):
        values, mats = inputs
        return complex_apply("ln,nm->lm", values, mats[0], mats[1]).astype(jnp.bfloat16)

    scattered = lax.map(scatter_one, (incident, t_matrices))
    grouped = scattered.reshape(G, GB, L, 2 * P_SIZE)
    members = jnp.arange(GB, dtype=jnp.int32)
    zero_seq = jnp.zeros((), hankel_rows.dtype)

    def group_near(inputs):
        group_values, group_offsets, group_slots = inputs

        def target_near(target):
            offset_row, position = target
            sequences = hankel_rows[offset_row[group_slots]]
            sequences = jnp.where((members != position)[:, None, None], sequences, zero_seq)
            mats = toeplitz_mats(sequences)
            return complex_apply("jln,jnm->lm", group_values, mats[:, 0], mats[:, 1])

        return lax.map(target_near, (group_offsets, members))

    near = lax.map(group_near, (grouped, offsets.reshape(G, GB, GB), lattice_slots.reshape(G, GB)))
    near = near.reshape(NB, L, 2 * P_SIZE)

    def expand_one(inputs):
        values, mats = inputs
        return complex_apply("ln,nq->lq", values, mats[0], mats[1])

    terms = lax.map(expand_one, (scattered, up_maps))
    expansion = jnp.sum(terms.reshape(G, GB, L, 2 * Q), axis=1).astype(jnp.bfloat16)
    group_ids = jnp.arange(G, dtype=jnp.int32)

    def incoming_one(inputs):
        row_maps, destination = inputs

        def add_source(total, source):
            values, mats, source_id = source
            term = complex_apply("ln,nq->lq", values, mats[0], mats[1])
            return total + jnp.where(source_id == destination, jnp.float32(0.0), term), None

        total, _ = lax.scan(add_source, jnp.zeros((L, 2 * Q), jnp.float32), (expansion, row_maps, group_ids))
        return total

    incoming = lax.map(incoming_one, (group_maps, group_ids)).astype(jnp.bfloat16)

    def far_one(inputs):
        mats, column = inputs
        values = incoming[column // GB]
        return complex_apply("lq,qp->lp", values, mats[0], mats[1])

    far = lax.map(far_one, (down_maps, jnp.arange(NB, dtype=jnp.int32)))
    return exciting + near + far
```

```python
import functools

import jax
import jax.numpy as jnp
from jax import lax
from jax.experimental import pallas as pl
from jax.experimental.pallas import tpu as pltpu
from jax.sharding import PartitionSpec as P

BF16 = jnp.bfloat16
F32 = jnp.float32
LANE = 128
ROWS = 16
GRP = 16
NY = 8
CELL = 4
MODES = 256
COEFS = 512


def dot(a, b):
    return jnp.dot(a, b, preferred_element_type=F32)


def paired(re, im):
    return jnp.concatenate(
        [jnp.concatenate([re, -im], axis=1), jnp.concatenate([im, re], axis=1)], axis=0
    )


def kernel(
    incident,
    exciting,
    t_maps,
    table,
    offsets,
    slots,
    up_maps,
    down_maps,
    group_maps,
    out,
    v_inc,
    v_exc,
    v_t,
    v_table,
    s_off,
    s_slot,
    v_up,
    v_down,
    v_gm,
    scat,
    near_out,
    near_in,
    u_out,
    u_in,
    e_out,
    e_in,
    g_out,
    g_in,
    p_out,
    p_in,
    q_out,
    q_in,
    i_all,
    load_sem,
    send_sem,
    recv_sem,
    near_send_sem,
):
    g = lax.axis_index("grp")
    b = lax.axis_index("body")
    y = b // CELL
    c = b % CELL

    loads = [
        pltpu.make_async_copy(src, dst, load_sem.at[k])
        for k, (src, dst) in enumerate(
            [
                (incident.at[0], v_inc),
                (t_maps.at[0], v_t),
                (offsets, s_off.at[pl.ds(0, 1)]),
                (slots, s_slot),
                (up_maps.at[0], v_up),
                (table, v_table),
                (group_maps.at[0], v_gm),
                (down_maps.at[0], v_down),
                (exciting.at[0], v_exc),
            ]
        )
    ]
    for copy in loads:
        copy.start()
    l_inc, l_t, l_off, l_slot, l_up, l_table, l_gm, l_down, l_exc = loads

    def y_peer(d):
        return {"grp": g, "body": lax.rem(y + d, NY) * CELL + c}

    def cell_peer(d):
        return {"grp": g, "body": y * CELL + lax.rem(c + d, CELL)}

    def grp_peer(d):
        return {"grp": lax.rem(g + d, GRP), "body": b}

    barrier = pltpu.get_barrier_semaphore()

    def greet(peer, count):
        def one(d, carry):
            pl.semaphore_signal(barrier, inc=1, device_id=peer(d), device_id_type=pl.DeviceIdType.MESH)
            return carry

        lax.fori_loop(1, count, one, 0)

    greet(cell_peer, CELL)
    greet(y_peer, NY)
    greet(grp_peer, GRP)

    def send(src, dst, phase, peer):
        return pltpu.make_async_remote_copy(
            src_ref=src,
            dst_ref=dst,
            send_sem=send_sem.at[phase],
            recv_sem=recv_sem.at[phase],
            device_id=peer,
            device_id_type=pl.DeviceIdType.MESH,
        )

    def send_all(count, make):
        def one(d, carry):
            make(d).start()
            return carry

        lax.fori_loop(1, count, one, 0)

    def wait_recv(ref, phase):
        pltpu.make_async_copy(ref, ref, recv_sem.at[phase]).wait()

    def wait_send(ref, phase):
        pltpu.make_async_copy(ref, ref, send_sem.at[phase]).wait()

    l_inc.wait()
    l_t.wait()
    x = v_inc[...]
    scattered = dot(
        paired(x[:, :MODES], x[:, MODES:]), v_t[...].reshape(2 * MODES, MODES)
    ).astype(BF16)
    scat[c] = scattered
    sr, si = scattered[:ROWS], scattered[ROWS:]
    own_pair = paired(sr, si)

    l_off.wait()
    pl.semaphore_wait(barrier, NY + CELL + GRP - 3)

    def send_off(d):
        return send(s_off.at[pl.ds(0, 1)], s_off.at[pl.ds(NY - d, 1)], 0, y_peer(d))

    def send_scat(d):
        return send(scat.at[c], scat.at[c], 1, cell_peer(d))

    send_all(NY, send_off)
    send_all(CELL, send_scat)

    l_up.wait()
    term = dot(own_pair, v_up[...].reshape(2 * MODES, COEFS)).astype(BF16)
    for t in range(4):
        u_out[t] = term[:, t * LANE : (t + 1) * LANE]

    def send_u(d):
        return send(u_out.at[lax.rem(y + d, NY) // 2], u_in.at[d - 1], 2, y_peer(d))

    send_all(NY, send_u)

    l_slot.wait()
    l_table.wait()
    wait_recv(scat.at[pl.ds(0, CELL - 1)], 1)
    wait_recv(s_off.at[pl.ds(0, NY - 1)], 0)
    lane = lax.broadcasted_iota(jnp.int32, (LANE, LANE), 1)
    sub = lax.broadcasted_iota(jnp.int32, (LANE, LANE), 0)
    wrapped = lane < sub

    def toeplitz(row):
        turned = [
            pltpu.roll(
                jnp.broadcast_to(row[:, k * LANE : (k + 1) * LANE], (LANE, LANE)),
                0,
                1,
                stride=1,
                stride_axis=0,
            )
            for k in range(4)
        ]
        wide = [
            jnp.where(wrapped, turned[k], turned[k + 1]).astype(BF16) for k in range(3)
        ]
        return jnp.concatenate(
            [
                jnp.concatenate([wide[1], wide[2]], axis=1),
                jnp.concatenate([wide[0], wide[1]], axis=1),
            ],
            axis=0,
        )

    def near_one(d):
        total = jnp.zeros((2 * ROWS, MODES), F32)
        for k in range(CELL):
            seq = v_table[s_off[d, s_slot[y * CELL + k]]].astype(F32)
            keep = jnp.logical_or(d != 0, k != c)
            seq = jnp.where(keep, seq, 0.0)
            mats = jnp.concatenate([toeplitz(seq[0:1]), toeplitz(seq[1:2])], axis=0)
            source = scat[k]
            total += dot(paired(source[:ROWS], source[ROWS:]), mats)
        return total

    def near_send(d):
        return pltpu.make_async_remote_copy(
            src_ref=near_out.at[d],
            dst_ref=near_in.at[d - 1],
            send_sem=near_send_sem,
            recv_sem=recv_sem.at[8],
            device_id=y_peer(d),
            device_id_type=pl.DeviceIdType.MESH,
        )

    def near_chunk(low, high):
        def one(d, carry):
            near_out[d] = near_one(d).astype(BF16)
            near_send(d).start()
            return carry

        lax.fori_loop(low, high, one, 0)

    near_chunk(1, 2)

    wait_recv(u_in, 2)
    e_sum = u_out[y // 2].astype(F32)
    for k in range(NY - 1):
        e_sum += u_in[k].astype(F32)
    e_out[...] = e_sum.astype(e_out.dtype)

    def send_e(d):
        return send(e_out, e_in.at[d - 1], 3, cell_peer(d))

    send_all(CELL, send_e)

    near_chunk(2, 3)

    wait_recv(e_in, 3)
    for k in range(CELL - 1):
        e_sum += e_in[k].astype(F32)
    own_block = lax.rem(b, 8)
    re_to = lax.rem(g, 8)
    im_to = lax.rem(g + 4, 8)
    re_part = pltpu.roll(e_sum[:ROWS], lax.rem(re_to - own_block + 8, 8) * 16, 1)
    im_part = pltpu.roll(e_sum[ROWS:], lax.rem(im_to - own_block + 8, 8) * 16, 1)
    block = lax.broadcasted_iota(jnp.int32, (ROWS, LANE), 1) // 16
    g_out[...] = jnp.where(block == re_to, re_part, im_part).astype(BF16)

    def send_g(d):
        return send(g_out, g_in.at[g], 4, grp_peer(d))

    send_all(GRP, send_g)
    g_in[g] = jnp.zeros((ROWS, LANE), BF16)

    near_chunk(3, 5)

    l_gm.wait()
    wait_recv(g_in.at[pl.ds(0, GRP - 1)], 4)
    res, ims = [], []
    for half in range(2):
        re = g_in[8 * half].astype(F32)
        im = re
        for k in range(1, 8):
            here = g_in[8 * half + k].astype(F32)
            re = jnp.where(block == k, here, re)
            im = jnp.where(block == (k + 4) % 8, here, im)
        res.append(re.astype(BF16))
        ims.append(pltpu.roll(im, 64, 1).astype(BF16))
    pair = paired(jnp.concatenate(res, axis=1), jnp.concatenate(ims, axis=1))
    gm = v_gm[...]
    mats = jnp.concatenate(
        [gm[:, 0].reshape(GRP * 16, COEFS), gm[:, 1].reshape(GRP * 16, COEFS)], axis=0
    )
    part = dot(pair, mats)
    for t in range(4):
        p_out[t] = part[:ROWS, t * LANE : (t + 1) * LANE].astype(BF16)
        p_out[4 + t] = part[ROWS:, t * LANE : (t + 1) * LANE].astype(BF16)

    def send_p(d):
        return send(p_out.at[lax.rem(y + d, NY)], p_in.at[d - 1], 5, y_peer(d))

    send_all(NY, send_p)

    near_chunk(5, 7)

    wait_recv(p_in, 5)
    q_sum = p_out[y].astype(F32)
    for k in range(NY - 1):
        q_sum += p_in[k].astype(F32)
    q_out[...] = q_sum.astype(q_out.dtype)

    def send_q(d):
        return send(q_out, q_in.at[d - 1], 6, cell_peer(d))

    send_all(CELL, send_q)

    near_chunk(7, 8)

    wait_recv(q_in, 6)
    for k in range(CELL - 1):
        q_sum += q_in[k].astype(F32)
    i_all[y] = q_sum.astype(BF16)

    def send_i(d):
        return send(i_all.at[y], i_all.at[y], 7, y_peer(d))

    send_all(NY, send_i)

    l_exc.wait()
    near = near_one(0)
    wait_recv(near_in, 8)
    for k in range(NY - 1):
        near += near_in[k].astype(F32)

    l_down.wait()
    wait_recv(i_all.at[pl.ds(0, NY - 1)], 7)
    incoming_re = jnp.concatenate([i_all[k] for k in range(4)], axis=1)
    incoming_im = jnp.concatenate([i_all[4 + k] for k in range(4)], axis=1)
    far = dot(paired(incoming_re, incoming_im), v_down[...].reshape(2 * COEFS, MODES))
    both = near + far
    out[0, :, :MODES] = v_exc[:, :MODES] + both[:ROWS]
    out[0, :, MODES:] = v_exc[:, MODES:] + both[ROWS:]

    wait_send(s_off.at[pl.ds(0, NY - 1)], 0)
    wait_send(scat.at[pl.ds(0, CELL - 1)], 1)
    wait_send(u_in, 2)
    wait_send(e_in, 3)
    wait_send(g_in.at[pl.ds(0, GRP - 1)], 4)
    wait_send(p_in, 5)
    wait_send(q_in, 6)
    wait_send(i_all.at[pl.ds(0, NY - 1)], 7)
    pltpu.make_async_copy(near_in, near_in, near_send_sem).wait()


def local(*args):
    anywhere = pl.BlockSpec(memory_space=pl.ANY)
    vmem = pltpu.VMEM
    return pl.pallas_call(
        kernel,
        out_shape=jax.ShapeDtypeStruct((1, ROWS, 2 * MODES), F32),
        in_specs=[anywhere] * 9,
        out_specs=pl.BlockSpec(memory_space=pltpu.VMEM),
        scratch_shapes=[
            vmem((ROWS, 2 * MODES), BF16),
            vmem((ROWS, 2 * MODES), F32),
            vmem((2, MODES, MODES), BF16),
            vmem((225, 2, 512), BF16),
            pltpu.SMEM((NY, 32), jnp.int32),
            pltpu.SMEM((32,), jnp.int32),
            vmem((2, MODES, COEFS), BF16),
            vmem((2, COEFS, MODES), BF16),
            vmem((GRP, 2, 16, COEFS), BF16),
            vmem((CELL, 2 * ROWS, MODES), BF16),
            vmem((NY, 2 * ROWS, MODES), BF16),
            vmem((NY - 1, 2 * ROWS, MODES), BF16),
            vmem((4, 2 * ROWS, LANE), BF16),
            vmem((NY - 1, 2 * ROWS, LANE), BF16),
            vmem((2 * ROWS, LANE), BF16),
            vmem((CELL - 1, 2 * ROWS, LANE), BF16),
            vmem((ROWS, LANE), BF16),
            vmem((GRP, ROWS, LANE), BF16),
            vmem((NY, ROWS, LANE), BF16),
            vmem((NY - 1, ROWS, LANE), BF16),
            vmem((ROWS, LANE), BF16),
            vmem((CELL - 1, ROWS, LANE), BF16),
            vmem((NY, ROWS, LANE), BF16),
            pltpu.SemaphoreType.DMA((9,)),
            pltpu.SemaphoreType.DMA((8,)),
            pltpu.SemaphoreType.DMA((9,)),
            pltpu.SemaphoreType.DMA,
        ],
        compiler_params=pltpu.CompilerParams(
            collective_id=0, has_side_effects=True, vmem_limit_bytes=32 * 1024 * 1024
        ),
        name="scatter_step",
    )(*args)


def solution(mesh):
    return jax.shard_map(
        local,
        mesh=mesh,
        in_specs=(
            P(("grp", "body"), None, None),
            P(("grp", "body"), None, None),
            P(("grp", "body"), None, None, None),
            P(),
            P(("grp", "body"), None),
            P("grp"),
            P(("grp", "body"), None, None, None),
            P(("grp", "body"), None, None, None),
            P("grp", None, None, "body", None),
        ),
        out_specs=P(("grp", "body"), None, None),
        check_vma=False,
    )
```

```python
import functools

import jax
import jax.numpy as jnp
from jax import lax
from jax.experimental import pallas as pl
from jax.experimental.pallas import tpu as pltpu
from jax.sharding import PartitionSpec as P

BF16 = jnp.bfloat16
F32 = jnp.float32
LANE = 128
ROWS = 16
GRP = 16
NY = 8
CELL = 4
MODES = 256
COEFS = 512


def dot(a, b):
    return jnp.dot(a, b, preferred_element_type=F32)


def paired(re, im):
    return jnp.concatenate(
        [jnp.concatenate([re, -im], axis=1), jnp.concatenate([im, re], axis=1)], axis=0
    )


def kernel(
    incident,
    exciting,
    t_maps,
    table,
    offsets,
    slots,
    up_maps,
    down_maps,
    group_maps,
    out,
    v_inc,
    v_exc,
    v_t,
    v_table,
    s_off,
    s_slot,
    v_up,
    v_down,
    v_gm,
    scat,
    near_out,
    near_in,
    u_out,
    u_in,
    e_out,
    e_in,
    g_out,
    g_in,
    p_out,
    p_in,
    q_out,
    q_in,
    i_all,
    load_sem,
    send_sem,
    recv_sem,
    near_send_sem,
):
    g = lax.axis_index("grp")
    b = lax.axis_index("body")
    y = b // CELL
    c = b % CELL

    loads = [
        pltpu.make_async_copy(src, dst, load_sem.at[k])
        for k, (src, dst) in enumerate(
            [
                (incident.at[0], v_inc),
                (t_maps.at[0], v_t),
                (offsets, s_off.at[pl.ds(0, 1)]),
                (slots, s_slot),
                (up_maps.at[0], v_up),
                (table, v_table),
                (group_maps.at[0], v_gm),
                (down_maps.at[0], v_down),
                (exciting.at[0], v_exc),
            ]
        )
    ]
    for copy in loads:
        copy.start()
    l_inc, l_t, l_off, l_slot, l_up, l_table, l_gm, l_down, l_exc = loads

    def y_peer(d):
        return {"grp": g, "body": lax.rem(y + d, NY) * CELL + c}

    def cell_peer(d):
        return {"grp": g, "body": y * CELL + lax.rem(c + d, CELL)}

    def grp_peer(d):
        return {"grp": lax.rem(g + d, GRP), "body": b}

    barrier = pltpu.get_barrier_semaphore()

    def greet(peer, count):
        def one(d, carry):
            pl.semaphore_signal(barrier, inc=1, device_id=peer(d), device_id_type=pl.DeviceIdType.MESH)
            return carry

        lax.fori_loop(1, count, one, 0)

    greet(cell_peer, CELL)
    greet(y_peer, NY)
    greet(grp_peer, GRP)

    def send(src, dst, phase, peer):
        return pltpu.make_async_remote_copy(
            src_ref=src,
            dst_ref=dst,
            send_sem=send_sem.at[phase],
            recv_sem=recv_sem.at[phase],
            device_id=peer,
            device_id_type=pl.DeviceIdType.MESH,
        )

    def send_all(count, make):
        def one(d, carry):
            make(d).start()
            return carry

        lax.fori_loop(1, count, one, 0)

    def wait_recv(ref, phase):
        pltpu.make_async_copy(ref, ref, recv_sem.at[phase]).wait()

    def wait_send(ref, phase):
        pltpu.make_async_copy(ref, ref, send_sem.at[phase]).wait()

    l_inc.wait()
    l_t.wait()
    x = v_inc[...]
    scattered = dot(
        paired(x[:, :MODES], x[:, MODES:]), v_t[...].reshape(2 * MODES, MODES)
    ).astype(BF16)
    scat[c] = scattered
    sr, si = scattered[:ROWS], scattered[ROWS:]
    own_pair = paired(sr, si)

    l_off.wait()
    pl.semaphore_wait(barrier, NY + CELL + GRP - 3)

    def send_off(d):
        return send(s_off.at[pl.ds(0, 1)], s_off.at[pl.ds(NY - d, 1)], 0, y_peer(d))

    def send_scat(d):
        return send(scat.at[c], scat.at[c], 1, cell_peer(d))

    send_all(NY, send_off)
    send_all(CELL, send_scat)

    l_up.wait()
    term = dot(own_pair, v_up[...].reshape(2 * MODES, COEFS)).astype(BF16)
    for t in range(4):
        u_out[t] = term[:, t * LANE : (t + 1) * LANE]

    def send_u(d):
        return send(u_out.at[lax.rem(y + d, NY) // 2], u_in.at[d - 1], 2, y_peer(d))

    send_all(NY, send_u)

    l_slot.wait()
    l_table.wait()
    wait_recv(scat.at[pl.ds(0, CELL - 1)], 1)
    wait_recv(s_off.at[pl.ds(0, NY - 1)], 0)
    lane = lax.broadcasted_iota(jnp.int32, (LANE, LANE), 1)
    sub = lax.broadcasted_iota(jnp.int32, (LANE, LANE), 0)
    wrapped = lane < sub

    def toeplitz(row):
        turned = [
            pltpu.roll(
                jnp.broadcast_to(row[:, k * LANE : (k + 1) * LANE], (LANE, LANE)),
                0,
                1,
                stride=1,
                stride_axis=0,
            )
            for k in range(4)
        ]
        wide = [
            jnp.where(wrapped, turned[k], turned[k + 1]).astype(BF16) for k in range(3)
        ]
        return jnp.concatenate(
            [
                jnp.concatenate([wide[1], wide[2]], axis=1),
                jnp.concatenate([wide[0], wide[1]], axis=1),
            ],
            axis=0,
        )

    def near_one(d):
        total = jnp.zeros((2 * ROWS, MODES), F32)
        for k in range(CELL):
            seq = v_table[s_off[d, s_slot[y * CELL + k]]].astype(F32)
            keep = jnp.logical_or(d != 0, k != c)
            seq = jnp.where(keep, seq, 0.0)
            mats = jnp.concatenate([toeplitz(seq[0:1]), toeplitz(seq[1:2])], axis=0)
            source = scat[k]
            total += dot(paired(source[:ROWS], source[ROWS:]), mats)
        return total

    def near_send(d):
        return pltpu.make_async_remote_copy(
            src_ref=near_out.at[d],
            dst_ref=near_in.at[d - 1],
            send_sem=near_send_sem,
            recv_sem=recv_sem.at[8],
            device_id=y_peer(d),
            device_id_type=pl.DeviceIdType.MESH,
        )

    def near_chunk(low, high):
        def one(d, carry):
            near_out[d] = near_one(d).astype(BF16)
            near_send(d).start()
            return carry

        lax.fori_loop(low, high, one, 0)

    near_chunk(1, 2)

    wait_recv(u_in, 2)
    e_sum = u_out[y // 2].astype(F32)
    for k in range(NY - 1):
        e_sum += u_in[k].astype(F32)
    e_out[...] = e_sum

    def send_e(d):
        return send(e_out, e_in.at[d - 1], 3, cell_peer(d))

    send_all(CELL, send_e)

    near_chunk(2, 3)

    wait_recv(e_in, 3)
    for k in range(CELL - 1):
        e_sum += e_in[k]
    own_block = lax.rem(b, 8)
    re_to = lax.rem(g, 8)
    im_to = lax.rem(g + 4, 8)
    re_part = pltpu.roll(e_sum[:ROWS], lax.rem(re_to - own_block + 8, 8) * 16, 1)
    im_part = pltpu.roll(e_sum[ROWS:], lax.rem(im_to - own_block + 8, 8) * 16, 1)
    block = lax.broadcasted_iota(jnp.int32, (ROWS, LANE), 1) // 16
    g_out[...] = jnp.where(block == re_to, re_part, im_part).astype(BF16)

    def send_g(d):
        return send(g_out, g_in.at[g], 4, grp_peer(d))

    send_all(GRP, send_g)
    g_in[g] = jnp.zeros((ROWS, LANE), BF16)

    near_chunk(3, 5)

    l_gm.wait()
    wait_recv(g_in.at[pl.ds(0, GRP - 1)], 4)
    res, ims = [], []
    for half in range(2):
        re = g_in[8 * half].astype(F32)
        im = re
        for k in range(1, 8):
            here = g_in[8 * half + k].astype(F32)
            re = jnp.where(block == k, here, re)
            im = jnp.where(block == (k + 4) % 8, here, im)
        res.append(re.astype(BF16))
        ims.append(pltpu.roll(im, 64, 1).astype(BF16))
    pair = paired(jnp.concatenate(res, axis=1), jnp.concatenate(ims, axis=1))
    gm = v_gm[...]
    mats = jnp.concatenate(
        [gm[:, 0].reshape(GRP * 16, COEFS), gm[:, 1].reshape(GRP * 16, COEFS)], axis=0
    )
    part = dot(pair, mats)
    for t in range(4):
        p_out[t] = part[:ROWS, t * LANE : (t + 1) * LANE]
        p_out[4 + t] = part[ROWS:, t * LANE : (t + 1) * LANE]

    def send_p(d):
        return send(p_out.at[lax.rem(y + d, NY)], p_in.at[d - 1], 5, y_peer(d))

    send_all(NY, send_p)

    near_chunk(5, 7)

    wait_recv(p_in, 5)
    q_sum = p_out[y]
    for k in range(NY - 1):
        q_sum += p_in[k]
    q_out[...] = q_sum

    def send_q(d):
        return send(q_out, q_in.at[d - 1], 6, cell_peer(d))

    send_all(CELL, send_q)

    near_chunk(7, 8)

    wait_recv(q_in, 6)
    for k in range(CELL - 1):
        q_sum += q_in[k]
    i_all[y] = q_sum.astype(BF16)

    def send_i(d):
        return send(i_all.at[y], i_all.at[y], 7, y_peer(d))

    send_all(NY, send_i)

    l_exc.wait()
    near = near_one(0)
    wait_recv(near_in, 8)
    for k in range(NY - 1):
        near += near_in[k].astype(F32)

    l_down.wait()
    wait_recv(i_all.at[pl.ds(0, NY - 1)], 7)
    incoming_re = jnp.concatenate([i_all[k] for k in range(4)], axis=1)
    incoming_im = jnp.concatenate([i_all[4 + k] for k in range(4)], axis=1)
    far = dot(paired(incoming_re, incoming_im), v_down[...].reshape(2 * COEFS, MODES))
    both = near + far
    out[0, :, :MODES] = v_exc[:, :MODES] + both[:ROWS]
    out[0, :, MODES:] = v_exc[:, MODES:] + both[ROWS:]

    wait_send(s_off.at[pl.ds(0, NY - 1)], 0)
    wait_send(scat.at[pl.ds(0, CELL - 1)], 1)
    wait_send(u_in, 2)
    wait_send(e_in, 3)
    wait_send(g_in.at[pl.ds(0, GRP - 1)], 4)
    wait_send(p_in, 5)
    wait_send(q_in, 6)
    wait_send(i_all.at[pl.ds(0, NY - 1)], 7)
    pltpu.make_async_copy(near_in, near_in, near_send_sem).wait()


def local(*args):
    anywhere = pl.BlockSpec(memory_space=pl.ANY)
    vmem = pltpu.VMEM
    return pl.pallas_call(
        kernel,
        out_shape=jax.ShapeDtypeStruct((1, ROWS, 2 * MODES), F32),
        in_specs=[anywhere] * 9,
        out_specs=pl.BlockSpec(memory_space=pltpu.VMEM),
        scratch_shapes=[
            vmem((ROWS, 2 * MODES), BF16),
            vmem((ROWS, 2 * MODES), F32),
            vmem((2, MODES, MODES), BF16),
            vmem((225, 2, 512), BF16),
            pltpu.SMEM((NY, 32), jnp.int32),
            pltpu.SMEM((32,), jnp.int32),
            vmem((2, MODES, COEFS), BF16),
            vmem((2, COEFS, MODES), BF16),
            vmem((GRP, 2, 16, COEFS), BF16),
            vmem((CELL, 2 * ROWS, MODES), BF16),
            vmem((NY, 2 * ROWS, MODES), BF16),
            vmem((NY - 1, 2 * ROWS, MODES), BF16),
            vmem((4, 2 * ROWS, LANE), BF16),
            vmem((NY - 1, 2 * ROWS, LANE), BF16),
            vmem((2 * ROWS, LANE), F32),
            vmem((CELL - 1, 2 * ROWS, LANE), F32),
            vmem((ROWS, LANE), BF16),
            vmem((GRP, ROWS, LANE), BF16),
            vmem((NY, ROWS, LANE), F32),
            vmem((NY - 1, ROWS, LANE), F32),
            vmem((ROWS, LANE), F32),
            vmem((CELL - 1, ROWS, LANE), F32),
            vmem((NY, ROWS, LANE), BF16),
            pltpu.SemaphoreType.DMA((9,)),
            pltpu.SemaphoreType.DMA((8,)),
            pltpu.SemaphoreType.DMA((9,)),
            pltpu.SemaphoreType.DMA,
        ],
        compiler_params=pltpu.CompilerParams(
            collective_id=0, has_side_effects=True, vmem_limit_bytes=63 * 1024 * 1024
        ),
        name="scatter_step",
    )(*args)


def solution(mesh):
    return jax.shard_map(
        local,
        mesh=mesh,
        in_specs=(
            P(("grp", "body"), None, None),
            P(("grp", "body"), None, None),
            P(("grp", "body"), None, None, None),
            P(),
            P(("grp", "body"), None),
            P("grp"),
            P(("grp", "body"), None, None, None),
            P(("grp", "body"), None, None, None),
            P("grp", None, None, "body", None),
        ),
        out_specs=P(("grp", "body"), None, None),
        check_vma=False,
    )
```

```python
import functools

import jax
import jax.numpy as jnp
from jax import lax
from jax.experimental import pallas as pl
from jax.experimental.pallas import tpu as pltpu
from jax.sharding import PartitionSpec as P

BF16 = jnp.bfloat16
F32 = jnp.float32
LANE = 128
ROWS = 16
HALF = 64
GRP = 16
NY = 8
CELL = 4
MODES = 256
COEFS = 512


def dot(a, b):
    return jnp.dot(a, b, preferred_element_type=F32)


def paired(re, im):
    return jnp.concatenate(
        [jnp.concatenate([re, -im], axis=1), jnp.concatenate([im, re], axis=1)], axis=0
    )


BODY_STEPS = [
    (dy, dc)
    for dy in (4, 3, 5, 2, 6, 1, 7, 0)
    for dc in (2, 3, 1, 0)
    if (dy, dc) != (0, 0)
]
Y_STEPS = (4, 3, 5, 2, 6, 1, 7)
CELL_STEPS = (2, 3, 1)
GRP_STEPS = sorted(
    [(dx, dz) for dx in range(4) for dz in range(4) if (dx, dz) != (0, 0)],
    key=lambda s: -(min(s[0], 4 - s[0]) + 2 * min(s[1], 4 - s[1])),
)


def kernel(
    incident,
    exciting,
    t_maps,
    table,
    offsets,
    slots,
    up_maps,
    down_maps,
    group_maps,
    out,
    v_inc,
    v_exc,
    v_t,
    v_table,
    s_off,
    s_slot,
    v_up,
    v_down,
    w_gm,
    scat,
    near_out,
    near_in,
    u_out,
    u_in,
    g_out,
    g_in,
    p_out,
    p_in,
    i_all,
    load_sem,
    send_sem,
    recv_sem,
):
    g = lax.axis_index("grp")
    b = lax.axis_index("body")
    y = b // CELL
    c = b % CELL
    gx = g // 4
    gz = g % 4

    def quarter(member):
        return group_maps.at[0, :, :, :, pl.ds(pl.multiple_of(member * LANE, LANE), LANE)]

    loads = [
        pltpu.make_async_copy(src, dst, load_sem.at[k])
        for k, (src, dst) in enumerate(
            [
                (incident.at[0], v_inc),
                (t_maps.at[0], v_t),
                (up_maps.at[0], v_up),
                (offsets, s_off.at[pl.ds(0, 1)]),
                (slots, s_slot),
                (table, v_table),
                (quarter(c), w_gm.at[:, :, c]),
                (down_maps.at[0], v_down),
                (exciting.at[0], v_exc),
            ]
        )
    ]
    for copy in loads:
        copy.start()
    l_inc, l_t, l_up, l_off, l_slot, l_table, l_gm, l_down, l_exc = loads

    def body_peer(step):
        dy, dc = step
        return {"grp": g, "body": lax.rem(y + dy, NY) * CELL + lax.rem(c + dc, CELL)}

    def y_peer(d):
        return body_peer((d, 0))

    def cell_peer(d):
        return body_peer((0, d))

    def grp_peer(step):
        dx, dz = step
        return {"grp": lax.rem(gx + dx, 4) * 4 + lax.rem(gz + dz, 4), "body": b}

    barrier = pltpu.get_barrier_semaphore()
    for peer in [grp_peer(s) for s in GRP_STEPS] + [body_peer(s) for s in BODY_STEPS]:
        pl.semaphore_signal(barrier, inc=1, device_id=peer, device_id_type=pl.DeviceIdType.MESH)

    def send(src, dst, phase, peer):
        pltpu.make_async_remote_copy(
            src_ref=src,
            dst_ref=dst,
            send_sem=send_sem.at[phase],
            recv_sem=recv_sem.at[phase],
            device_id=peer,
            device_id_type=pl.DeviceIdType.MESH,
        ).start()

    def wait_recv(ref, phase):
        pltpu.make_async_copy(ref, ref, recv_sem.at[phase]).wait()

    def wait_send(ref, phase):
        pltpu.make_async_copy(ref, ref, send_sem.at[phase]).wait()

    l_inc.wait()
    l_t.wait()
    x = v_inc[...]
    scattered = dot(
        paired(x[:, :MODES], x[:, MODES:]), v_t[...].reshape(2 * MODES, MODES)
    ).astype(BF16)
    scat[c] = scattered
    own_pair = paired(scattered[:ROWS], scattered[ROWS:])

    l_up.wait()
    term = dot(own_pair, v_up[...].reshape(2 * MODES, COEFS))
    low = lax.broadcasted_iota(jnp.int32, (ROWS, LANE), 1) < HALF
    for t in range(4):
        re = term[:ROWS, t * LANE : (t + 1) * LANE]
        im = term[ROWS:, t * LANE : (t + 1) * LANE]
        u_out[2 * t] = jnp.where(low, re, pltpu.roll(im, HALF, 1)).astype(BF16)
        u_out[2 * t + 1] = jnp.where(low, pltpu.roll(re, HALF, 1), im).astype(BF16)
    l_off.wait()

    pl.semaphore_wait(barrier, len(BODY_STEPS) + len(GRP_STEPS))
    for k, step in enumerate(BODY_STEPS):
        send(u_out.at[lax.rem(y + step[0], NY)], u_in.at[k], 2, body_peer(step))
    for d in Y_STEPS:
        send(s_off.at[pl.ds(0, 1)], s_off.at[pl.ds(NY - d, 1)], 0, y_peer(d))
    for d in CELL_STEPS:
        send(scat.at[c], scat.at[c], 1, cell_peer(d))
    for d in CELL_STEPS:
        send(quarter(lax.rem(c + d, CELL)), w_gm.at[:, :, c], 3, cell_peer(d))

    wait_recv(u_in, 2)
    e_sum = u_out[y].astype(F32)
    for k in range(len(BODY_STEPS)):
        e_sum += u_in[k].astype(F32)
    g_out[...] = e_sum.astype(BF16)
    for step in GRP_STEPS:
        send(g_out, g_in.at[g], 4, grp_peer(step))
    g_in[g] = jnp.zeros((ROWS, LANE), BF16)

    l_slot.wait()
    l_table.wait()
    wait_recv(scat.at[pl.ds(0, CELL - 1)], 1)
    wait_recv(s_off.at[pl.ds(0, NY - 1)], 0)
    lane = lax.broadcasted_iota(jnp.int32, (LANE, LANE), 1)
    sub = lax.broadcasted_iota(jnp.int32, (LANE, LANE), 0)
    wrapped = lane < sub

    def toeplitz(row):
        turned = [
            pltpu.roll(
                jnp.broadcast_to(row[:, k * LANE : (k + 1) * LANE], (LANE, LANE)),
                0,
                1,
                stride=1,
                stride_axis=0,
            )
            for k in range(4)
        ]
        wide = [
            jnp.where(wrapped, turned[k], turned[k + 1]).astype(BF16) for k in range(3)
        ]
        return jnp.concatenate(
            [
                jnp.concatenate([wide[1], wide[2]], axis=1),
                jnp.concatenate([wide[0], wide[1]], axis=1),
            ],
            axis=0,
        )

    def near_one(d):
        total = jnp.zeros((2 * ROWS, MODES), F32)
        for k in range(CELL):
            seq = v_table[s_off[d, s_slot[y * CELL + k]]].astype(F32)
            keep = jnp.logical_or(d != 0, k != c)
            seq = jnp.where(keep, seq, 0.0)
            mats = jnp.concatenate([toeplitz(seq[0:1]), toeplitz(seq[1:2])], axis=0)
            source = scat[k]
            total += dot(paired(source[:ROWS], source[ROWS:]), mats)
        return total

    def near_chunk(low, high):
        def one(d, carry):
            near_out[d] = near_one(d).astype(BF16)
            send(near_out.at[d], near_in.at[d - 1], 6, y_peer(d))
            return carry

        lax.fori_loop(low, high, one, 0)

    near_chunk(1, NY)

    l_gm.wait()
    wait_recv(w_gm.at[:, :, pl.ds(0, CELL - 1)], 3)
    wait_recv(g_in.at[pl.ds(0, GRP - 1)], 4)
    tops, bottoms = [], []
    for h in range(GRP):
        pair = g_in[h].astype(F32)
        tops.append(jnp.where(low, pair, -pair).astype(BF16))
        bottoms.append(pltpu.roll(pair, HALF, 1).astype(BF16))
    left = jnp.concatenate(
        [jnp.concatenate(tops, axis=1), jnp.concatenate(bottoms, axis=1)], axis=0
    )
    p_sum = dot(left, w_gm[...].reshape(GRP * LANE, LANE))
    p_out[...] = p_sum.astype(BF16)
    for k, d in enumerate(Y_STEPS):
        send(p_out, p_in.at[k], 5, y_peer(d))

    near = near_one(0)
    wait_recv(p_in, 5)
    for k in range(NY - 1):
        p_sum += p_in[k].astype(F32)
    i_all[c] = p_sum.astype(BF16)
    for d in CELL_STEPS:
        send(i_all.at[c], i_all.at[c], 7, cell_peer(d))

    wait_recv(near_in, 6)
    for k in range(NY - 1):
        near += near_in[k].astype(F32)
    l_exc.wait()
    near_re = v_exc[:, :MODES] + near[:ROWS]
    near_im = v_exc[:, MODES:] + near[ROWS:]

    l_down.wait()
    wait_recv(i_all.at[pl.ds(0, CELL - 1)], 7)
    incoming_re = jnp.concatenate([i_all[k][:ROWS] for k in range(CELL)], axis=1)
    incoming_im = jnp.concatenate([i_all[k][ROWS:] for k in range(CELL)], axis=1)
    far = dot(paired(incoming_re, incoming_im), v_down[...].reshape(2 * COEFS, MODES))
    out[0, :, :MODES] = near_re + far[:ROWS]
    out[0, :, MODES:] = near_im + far[ROWS:]

    wait_send(s_off.at[pl.ds(0, NY - 1)], 0)
    wait_send(scat.at[pl.ds(0, CELL - 1)], 1)
    wait_send(u_in, 2)
    wait_send(w_gm.at[:, :, pl.ds(0, CELL - 1)], 3)
    wait_send(g_in.at[pl.ds(0, GRP - 1)], 4)
    wait_send(p_in, 5)
    wait_send(near_in, 6)
    wait_send(i_all.at[pl.ds(0, CELL - 1)], 7)


def local(*args):
    anywhere = pl.BlockSpec(memory_space=pl.ANY)
    vmem = pltpu.VMEM
    return pl.pallas_call(
        kernel,
        out_shape=jax.ShapeDtypeStruct((1, ROWS, 2 * MODES), F32),
        in_specs=[anywhere] * 9,
        out_specs=pl.BlockSpec(memory_space=pltpu.VMEM),
        scratch_shapes=[
            vmem((ROWS, 2 * MODES), BF16),
            vmem((ROWS, 2 * MODES), F32),
            vmem((2, MODES, MODES), BF16),
            vmem((225, 2, 512), BF16),
            pltpu.SMEM((NY, 32), jnp.int32),
            pltpu.SMEM((32,), jnp.int32),
            vmem((2, MODES, COEFS), BF16),
            vmem((2, COEFS, MODES), BF16),
            vmem((GRP, 2, CELL, 16, LANE), BF16),
            vmem((CELL, 2 * ROWS, MODES), BF16),
            vmem((NY, 2 * ROWS, MODES), BF16),
            vmem((NY - 1, 2 * ROWS, MODES), BF16),
            vmem((NY, ROWS, LANE), BF16),
            vmem((NY * CELL - 1, ROWS, LANE), BF16),
            vmem((ROWS, LANE), BF16),
            vmem((GRP, ROWS, LANE), BF16),
            vmem((2 * ROWS, LANE), BF16),
            vmem((NY - 1, 2 * ROWS, LANE), BF16),
            vmem((CELL, 2 * ROWS, LANE), BF16),
            pltpu.SemaphoreType.DMA((9,)),
            pltpu.SemaphoreType.DMA((8,)),
            pltpu.SemaphoreType.DMA((8,)),
        ],
        compiler_params=pltpu.CompilerParams(
            collective_id=0, has_side_effects=True, vmem_limit_bytes=63 * 1024 * 1024
        ),
        name="scatter_step",
    )(*args)


def solution(mesh):
    return jax.shard_map(
        local,
        mesh=mesh,
        in_specs=(
            P(("grp", "body"), None, None),
            P(("grp", "body"), None, None),
            P(("grp", "body"), None, None, None),
            P(),
            P(("grp", "body"), None),
            P("grp"),
            P(("grp", "body"), None, None, None),
            P(("grp", "body"), None, None, None),
            P("grp", None, None, "body", None),
        ),
        out_specs=P(("grp", "body"), None, None),
        check_vma=False,
    )
```

```python
import functools

import jax
import jax.numpy as jnp
from jax import lax
from jax.experimental import pallas as pl
from jax.experimental.pallas import tpu as pltpu
from jax.sharding import PartitionSpec as P

BF16 = jnp.bfloat16
F32 = jnp.float32
LANE = 128
ROWS = 16
HALF = 64
GRP = 16
NY = 8
CELL = 4
MODES = 256
COEFS = 512


def dot(a, b):
    return jnp.dot(a, b, preferred_element_type=F32)


def paired(re, im):
    return jnp.concatenate(
        [jnp.concatenate([re, -im], axis=1), jnp.concatenate([im, re], axis=1)], axis=0
    )


BODY_STEPS = [
    (dy, dc)
    for dy in (4, 3, 5, 2, 6, 1, 7, 0)
    for dc in (2, 3, 1, 0)
    if (dy, dc) != (0, 0)
]
Y_STEPS = (4, 3, 5, 2, 6, 1, 7)
CELL_STEPS = (2, 3, 1)
GRP_STEPS = sorted(
    [(dx, dz) for dx in range(4) for dz in range(4) if (dx, dz) != (0, 0)],
    key=lambda s: -(min(s[0], 4 - s[0]) + 2 * min(s[1], 4 - s[1])),
)


def kernel(
    incident,
    exciting,
    t_maps,
    table,
    offsets,
    slots,
    up_maps,
    down_maps,
    group_maps,
    out,
    v_inc,
    v_exc,
    v_t,
    v_table,
    s_off,
    s_slot,
    v_up,
    v_down,
    w_gm,
    scat,
    near_out,
    near_in,
    u_out,
    u_in,
    g_out,
    g_in,
    p_out,
    p_in,
    i_all,
    load_sem,
    send_sem,
    recv_sem,
):
    g = lax.axis_index("grp")
    b = lax.axis_index("body")
    y = b // CELL
    c = b % CELL
    gx = g // 4
    gz = g % 4

    def quarter(member):
        return group_maps.at[0, :, :, :, pl.ds(pl.multiple_of(member * LANE, LANE), LANE)]

    loads = [
        pltpu.make_async_copy(src, dst, load_sem.at[k])
        for k, (src, dst) in enumerate(
            [
                (incident.at[0], v_inc),
                (t_maps.at[0], v_t),
                (up_maps.at[0], v_up),
                (offsets, s_off.at[pl.ds(0, 1)]),
                (slots, s_slot),
                (table, v_table),
                (quarter(c), w_gm.at[:, :, c]),
                (down_maps.at[0], v_down),
                (exciting.at[0], v_exc),
            ]
        )
    ]
    for copy in loads:
        copy.start()
    l_inc, l_t, l_up, l_off, l_slot, l_table, l_gm, l_down, l_exc = loads

    def body_peer(step):
        dy, dc = step
        return {"grp": g, "body": lax.rem(y + dy, NY) * CELL + lax.rem(c + dc, CELL)}

    def y_peer(d):
        return body_peer((d, 0))

    def cell_peer(d):
        return body_peer((0, d))

    def grp_peer(step):
        dx, dz = step
        return {"grp": lax.rem(gx + dx, 4) * 4 + lax.rem(gz + dz, 4), "body": b}

    barrier = pltpu.get_barrier_semaphore()
    for peer in [grp_peer(s) for s in GRP_STEPS] + [body_peer(s) for s in BODY_STEPS]:
        pl.semaphore_signal(barrier, inc=1, device_id=peer, device_id_type=pl.DeviceIdType.MESH)

    def send(src, dst, phase, peer):
        pltpu.make_async_remote_copy(
            src_ref=src,
            dst_ref=dst,
            send_sem=send_sem.at[phase],
            recv_sem=recv_sem.at[phase],
            device_id=peer,
            device_id_type=pl.DeviceIdType.MESH,
        ).start()

    def wait_recv(ref, phase):
        pltpu.make_async_copy(ref, ref, recv_sem.at[phase]).wait()

    def wait_send(ref, phase):
        pltpu.make_async_copy(ref, ref, send_sem.at[phase]).wait()

    l_inc.wait()
    l_t.wait()
    x = v_inc[...]
    scattered = dot(
        paired(x[:, :MODES], x[:, MODES:]), v_t[...].reshape(2 * MODES, MODES)
    ).astype(BF16)
    scat[c] = scattered
    own_pair = paired(scattered[:ROWS], scattered[ROWS:])

    l_up.wait()
    term = dot(own_pair, v_up[...].reshape(2 * MODES, COEFS))
    low = lax.broadcasted_iota(jnp.int32, (ROWS, LANE), 1) < HALF
    for t in range(4):
        re = term[:ROWS, t * LANE : (t + 1) * LANE]
        im = term[ROWS:, t * LANE : (t + 1) * LANE]
        u_out[2 * t] = jnp.where(low, re, pltpu.roll(im, HALF, 1)).astype(BF16)
        u_out[2 * t + 1] = jnp.where(low, pltpu.roll(re, HALF, 1), im).astype(BF16)
    l_off.wait()

    pl.semaphore_wait(barrier, len(BODY_STEPS) + len(GRP_STEPS))
    for k, step in enumerate(BODY_STEPS):
        send(u_out.at[lax.rem(y + step[0], NY)], u_in.at[k], 2, body_peer(step))
    for d in Y_STEPS:
        send(s_off.at[pl.ds(0, 1)], s_off.at[pl.ds(NY - d, 1)], 0, y_peer(d))
    for d in CELL_STEPS:
        send(scat.at[c], scat.at[c], 1, cell_peer(d))
    for d in CELL_STEPS:
        send(quarter(lax.rem(c + d, CELL)), w_gm.at[:, :, c], 3, cell_peer(d))

    wait_recv(u_in, 2)
    e_sum = u_out[y].astype(F32)
    for k in range(len(BODY_STEPS)):
        e_sum += u_in[k].astype(F32)
    g_out[...] = e_sum.astype(BF16)
    for step in GRP_STEPS:
        send(g_out, g_in.at[g], 4, grp_peer(step))
    g_in[g] = jnp.zeros((ROWS, LANE), BF16)

    l_slot.wait()
    l_table.wait()
    wait_recv(scat.at[pl.ds(0, CELL - 1)], 1)
    wait_recv(s_off.at[pl.ds(0, NY - 1)], 0)
    lane = lax.broadcasted_iota(jnp.int32, (LANE, LANE), 1)
    sub = lax.broadcasted_iota(jnp.int32, (LANE, LANE), 0)
    wrapped = lane < sub

    def toeplitz(row):
        turned = [
            pltpu.roll(
                jnp.broadcast_to(row[:, k * LANE : (k + 1) * LANE], (LANE, LANE)),
                0,
                1,
                stride=1,
                stride_axis=0,
            )
            for k in range(4)
        ]
        wide = [
            jnp.where(wrapped, turned[k], turned[k + 1]).astype(BF16) for k in range(3)
        ]
        return jnp.concatenate(
            [
                jnp.concatenate([wide[1], wide[2]], axis=1),
                jnp.concatenate([wide[0], wide[1]], axis=1),
            ],
            axis=0,
        )

    def near_one(d):
        total = jnp.zeros((2 * ROWS, MODES), F32)
        for k in range(CELL):
            seq = v_table[s_off[d, s_slot[y * CELL + k]]].astype(F32)
            keep = jnp.logical_or(d != 0, k != c)
            seq = jnp.where(keep, seq, 0.0)
            mats = jnp.concatenate([toeplitz(seq[0:1]), toeplitz(seq[1:2])], axis=0)
            source = scat[k]
            total += dot(paired(source[:ROWS], source[ROWS:]), mats)
        return total

    def near_chunk(low, high):
        def one(d, carry):
            near_out[d] = near_one(d).astype(BF16)
            send(near_out.at[d], near_in.at[d - 1], 6, y_peer(d))
            return carry

        lax.fori_loop(low, high, one, 0)

    near_chunk(1, NY)

    l_gm.wait()
    wait_recv(w_gm.at[:, :, pl.ds(0, CELL - 1)], 3)
    wait_recv(g_in.at[pl.ds(0, GRP - 1)], 4)
    tops, bottoms = [], []
    for h in range(GRP):
        pair = g_in[h].astype(F32)
        tops.append(jnp.where(low, pair, -pair).astype(BF16))
        bottoms.append(pltpu.roll(pair, HALF, 1).astype(BF16))
    left = jnp.concatenate(
        [jnp.concatenate(tops, axis=1), jnp.concatenate(bottoms, axis=1)], axis=0
    )
    p_sum = dot(left, w_gm[...].reshape(GRP * LANE, LANE))
    p_out[...] = p_sum.astype(BF16)
    for k, d in enumerate(Y_STEPS):
        send(p_out, p_in.at[k], 5, y_peer(d))

    near = near_one(0)
    wait_recv(p_in, 5)
    for k in range(NY - 1):
        p_sum += p_in[k].astype(F32)
    i_all[c] = p_sum.astype(BF16)
    for d in CELL_STEPS:
        send(i_all.at[c], i_all.at[c], 7, cell_peer(d))

    wait_recv(near_in, 6)
    for k in range(NY - 1):
        near += near_in[k].astype(F32)
    l_exc.wait()
    near_re = v_exc[:, :MODES] + near[:ROWS]
    near_im = v_exc[:, MODES:] + near[ROWS:]

    l_down.wait()
    wait_recv(i_all.at[pl.ds(0, CELL - 1)], 7)
    incoming_re = jnp.concatenate([i_all[k][:ROWS] for k in range(CELL)], axis=1)
    incoming_im = jnp.concatenate([i_all[k][ROWS:] for k in range(CELL)], axis=1)
    far = dot(paired(incoming_re, incoming_im), v_down[...].reshape(2 * COEFS, MODES))
    out[0, :, :MODES] = near_re + far[:ROWS]
    out[0, :, MODES:] = near_im + far[ROWS:]

    wait_send(s_off.at[pl.ds(0, NY - 1)], 0)
    wait_send(scat.at[pl.ds(0, CELL - 1)], 1)
    wait_send(u_in, 2)
    wait_send(w_gm.at[:, :, pl.ds(0, CELL - 1)], 3)
    wait_send(g_in.at[pl.ds(0, GRP - 1)], 4)
    wait_send(p_in, 5)
    wait_send(near_in, 6)
    wait_send(i_all.at[pl.ds(0, CELL - 1)], 7)


def local(*args):
    anywhere = pl.BlockSpec(memory_space=pl.ANY)
    vmem = pltpu.VMEM
    return pl.pallas_call(
        kernel,
        out_shape=jax.ShapeDtypeStruct((1, ROWS, 2 * MODES), F32),
        in_specs=[anywhere] * 9,
        out_specs=pl.BlockSpec(memory_space=pltpu.VMEM),
        scratch_shapes=[
            vmem((ROWS, 2 * MODES), BF16),
            vmem((ROWS, 2 * MODES), F32),
            vmem((2, MODES, MODES), BF16),
            vmem((225, 2, 512), BF16),
            pltpu.SMEM((NY, 32), jnp.int32),
            pltpu.SMEM((32,), jnp.int32),
            vmem((2, MODES, COEFS), BF16),
            vmem((2, COEFS, MODES), BF16),
            vmem((GRP, 2, CELL, 16, LANE), BF16),
            vmem((CELL, 2 * ROWS, MODES), BF16),
            vmem((NY, 2 * ROWS, MODES), BF16),
            vmem((NY - 1, 2 * ROWS, MODES), BF16),
            vmem((NY, ROWS, LANE), BF16),
            vmem((NY * CELL - 1, ROWS, LANE), BF16),
            vmem((ROWS, LANE), BF16),
            vmem((GRP, ROWS, LANE), BF16),
            vmem((2 * ROWS, LANE), BF16),
            vmem((NY - 1, 2 * ROWS, LANE), BF16),
            vmem((CELL, 2 * ROWS, LANE), BF16),
            pltpu.SemaphoreType.DMA((9,)),
            pltpu.SemaphoreType.DMA((8,)),
            pltpu.SemaphoreType.DMA((8,)),
        ],
        compiler_params=pltpu.CompilerParams(
            collective_id=0, has_side_effects=True, vmem_limit_bytes=32 * 1024 * 1024
        ),
        name="scatter_step",
    )(*[pltpu.with_memory_space_constraint(a, pltpu.HBM) for a in args])


def solution(mesh):
    return jax.shard_map(
        local,
        mesh=mesh,
        in_specs=(
            P(("grp", "body"), None, None),
            P(("grp", "body"), None, None),
            P(("grp", "body"), None, None, None),
            P(),
            P(("grp", "body"), None),
            P("grp"),
            P(("grp", "body"), None, None, None),
            P(("grp", "body"), None, None, None),
            P("grp", None, None, "body", None),
        ),
        out_specs=P(("grp", "body"), None, None),
        check_vma=False,
    )
```

```python
import functools

import jax
import jax.numpy as jnp
from jax import lax
from jax.experimental import pallas as pl
from jax.experimental.pallas import tpu as pltpu
from jax.sharding import PartitionSpec as P

BF16 = jnp.bfloat16
F32 = jnp.float32
LANE = 128
ROWS = 16
HALF = 64
GRP = 16
NY = 8
CELL = 4
MODES = 256
COEFS = 512


def dot(a, b):
    return jnp.dot(a, b, preferred_element_type=F32)


def paired(re, im):
    return jnp.concatenate(
        [jnp.concatenate([re, -im], axis=1), jnp.concatenate([im, re], axis=1)], axis=0
    )


BODY_STEPS = [
    (dy, dc)
    for dy in (4, 3, 5, 2, 6, 1, 7, 0)
    for dc in (2, 3, 1, 0)
    if (dy, dc) != (0, 0)
]
FAR_BODY = 12
Y_STEPS = (4, 3, 5, 2, 6, 1, 7)
CELL_STEPS = (2, 3, 1)
CORE_STEPS = [(dy, dc) for dy in (4, 3, 5, 2, 6, 1, 7, 0) for dc in (2, 0) if (dy, dc) != (0, 0)]
FAR_CORE = 6
GRP_STEPS = sorted(
    [(dx, dz) for dx in range(4) for dz in range(4) if (dx, dz) != (0, 0)],
    key=lambda s: -(min(s[0], 4 - s[0]) + 2 * min(s[1], 4 - s[1])),
)
FAR_GRP = 4


def grp_hops(step):
    return min(step[0], 4 - step[0]) + 2 * min(step[1], 4 - step[1])


def body_hops(step):
    return min(step[0], NY - step[0]) + (0, 0.5, 1, 0.5)[step[1]]


def kernel(
    incident,
    exciting,
    t_maps,
    table,
    offsets,
    slots,
    up_maps,
    down_maps,
    group_maps,
    out,
    v_inc,
    v_exc,
    v_t,
    v_table,
    s_off,
    s_slot,
    v_up,
    v_down,
    w_gm,
    scat,
    near_out,
    near_in,
    u_out,
    u_in,
    g_out,
    g_in,
    p_out,
    p_in,
    i_all,
    load_sem,
    send_sem,
    recv_sem,
):
    g = lax.axis_index("grp")
    b = lax.axis_index("body")
    y = b // CELL
    c = b % CELL
    gx = g // 4
    gz = g % 4

    def quarter(member):
        return group_maps.at[0, :, :, :, pl.ds(pl.multiple_of(member * LANE, LANE), LANE)]

    def body_peer(step):
        dy, dc = step
        return {"grp": g, "body": lax.rem(y + dy, NY) * CELL + lax.rem(c + dc, CELL)}

    def y_peer(d):
        return body_peer((d, 0))

    def cell_peer(d):
        return body_peer((0, d))

    def grp_peer(step):
        dx, dz = step
        return {"grp": lax.rem(gx + dx, 4) * 4 + lax.rem(gz + dz, 4), "body": b}

    barrier = pltpu.get_barrier_semaphore()
    greeted = [(grp_hops(s), grp_peer, s) for s in GRP_STEPS]
    greeted += [(body_hops(s), body_peer, s) for s in BODY_STEPS]
    for _, peer, step in sorted(greeted, key=lambda entry: -entry[0]):
        pl.semaphore_signal(
            barrier, inc=1, device_id=peer(step), device_id_type=pl.DeviceIdType.MESH
        )

    loads = [
        pltpu.make_async_copy(src, dst, load_sem.at[k])
        for k, (src, dst) in enumerate(
            [
                (incident.at[0], v_inc),
                (t_maps.at[0], v_t),
                (up_maps.at[0], v_up),
                (offsets, s_off.at[pl.ds(0, 1)]),
                (slots, s_slot),
                (table, v_table),
                (quarter(c), w_gm.at[:, :, c]),
                (down_maps.at[0], v_down),
                (exciting.at[0], v_exc),
            ]
        )
    ]
    for copy in loads:
        copy.start()
    l_inc, l_t, l_up, l_off, l_slot, l_table, l_gm, l_down, l_exc = loads

    def send(src, dst, phase, peer):
        pltpu.make_async_remote_copy(
            src_ref=src,
            dst_ref=dst,
            send_sem=send_sem.at[phase],
            recv_sem=recv_sem.at[phase],
            device_id=peer,
            device_id_type=pl.DeviceIdType.MESH,
        ).start()

    def wait_recv(ref, phase):
        pltpu.make_async_copy(ref, ref, recv_sem.at[phase]).wait()

    def wait_send(ref, phase):
        pltpu.make_async_copy(ref, ref, send_sem.at[phase]).wait()

    l_inc.wait()
    l_t.wait()
    x = v_inc[...]
    scattered = dot(
        paired(x[:, :MODES], x[:, MODES:]), v_t[...].reshape(2 * MODES, MODES)
    ).astype(BF16)
    scat[c] = scattered
    own_pair = paired(scattered[:ROWS], scattered[ROWS:])

    l_up.wait()
    term = dot(own_pair, v_up[...].reshape(2 * MODES, COEFS))
    low = lax.broadcasted_iota(jnp.int32, (ROWS, LANE), 1) < HALF
    for t in range(4):
        re = term[:ROWS, t * LANE : (t + 1) * LANE]
        im = term[ROWS:, t * LANE : (t + 1) * LANE]
        u_out[2 * t] = jnp.where(low, re, pltpu.roll(im, HALF, 1)).astype(BF16)
        u_out[2 * t + 1] = jnp.where(low, pltpu.roll(re, HALF, 1), im).astype(BF16)
    l_off.wait()

    pl.semaphore_wait(barrier, len(BODY_STEPS) + len(GRP_STEPS))
    for k, step in enumerate(BODY_STEPS):
        phase = 2 if k < FAR_BODY else 8
        send(u_out.at[lax.rem(y + step[0], NY)], u_in.at[k], phase, body_peer(step))
    for d in Y_STEPS:
        send(s_off.at[pl.ds(0, 1)], s_off.at[pl.ds(NY - d, 1)], 0, y_peer(d))
    for d in CELL_STEPS:
        send(scat.at[c], scat.at[c], 1, cell_peer(d))
    for d in CELL_STEPS:
        send(quarter(lax.rem(c + d, CELL)), w_gm.at[:, :, c], 3, cell_peer(d))

    near_body = u_in.at[pl.ds(FAR_BODY, len(BODY_STEPS) - FAR_BODY)]
    far_body = u_in.at[pl.ds(0, FAR_BODY)]
    e_sum = u_out[y].astype(F32)
    wait_recv(near_body, 8)
    for k in range(FAR_BODY, len(BODY_STEPS)):
        e_sum += u_in[k].astype(F32)
    wait_recv(far_body, 2)
    for k in range(FAR_BODY):
        e_sum += u_in[k].astype(F32)
    g_out[...] = e_sum.astype(BF16)
    for step in GRP_STEPS:
        send(g_out, g_in.at[g], 4 if step[1] == 2 else 9, grp_peer(step))
    g_in[g] = jnp.zeros((ROWS, LANE), BF16)

    l_slot.wait()
    l_table.wait()
    wait_recv(scat.at[pl.ds(0, CELL - 1)], 1)
    wait_recv(s_off.at[pl.ds(0, NY - 1)], 0)
    lane = lax.broadcasted_iota(jnp.int32, (LANE, LANE), 1)
    sub = lax.broadcasted_iota(jnp.int32, (LANE, LANE), 0)
    wrapped = lane < sub

    def toeplitz(row):
        turned = [
            pltpu.roll(
                jnp.broadcast_to(row[:, k * LANE : (k + 1) * LANE], (LANE, LANE)),
                0,
                1,
                stride=1,
                stride_axis=0,
            )
            for k in range(4)
        ]
        wide = [
            jnp.where(wrapped, turned[k], turned[k + 1]).astype(BF16) for k in range(3)
        ]
        return jnp.concatenate(
            [
                jnp.concatenate([wide[1], wide[2]], axis=1),
                jnp.concatenate([wide[0], wide[1]], axis=1),
            ],
            axis=0,
        )

    def near_one(d):
        total = jnp.zeros((2 * ROWS, MODES), F32)
        for k in range(CELL):
            seq = v_table[s_off[d, s_slot[y * CELL + k]]].astype(F32)
            keep = jnp.logical_or(d != 0, k != c)
            seq = jnp.where(keep, seq, 0.0)
            mats = jnp.concatenate([toeplitz(seq[0:1]), toeplitz(seq[1:2])], axis=0)
            source = scat[k]
            total += dot(paired(source[:ROWS], source[ROWS:]), mats)
        return total

    def near_chunk(low, high):
        def one(d, carry):
            near_out[d] = near_one(d).astype(BF16)
            send(near_out.at[d], near_in.at[d - 1], 6, y_peer(d))
            return carry

        lax.fori_loop(low, high, one, 0)

    near_chunk(1, NY)

    l_gm.wait()
    wait_recv(w_gm.at[:, :, pl.ds(0, CELL - 1)], 3)

    def from_groups(z_steps):
        tops, bottoms, mats = [], [], []
        for dz in z_steps:
            for x_at in range(4):
                h = x_at * 4 + lax.rem(gz + dz, 4)
                pair = g_in[h].astype(F32)
                tops.append(jnp.where(low, pair, -pair).astype(BF16))
                bottoms.append(pltpu.roll(pair, HALF, 1).astype(BF16))
                mats.append(w_gm[h].reshape(LANE, LANE))
        left = jnp.concatenate(
            [jnp.concatenate(tops, axis=1), jnp.concatenate(bottoms, axis=1)], axis=0
        )
        return dot(left, jnp.concatenate(mats, axis=0))

    near_grp = g_in.at[pl.ds(0, GRP - 1 - FAR_GRP)]
    far_grp = g_in.at[pl.ds(0, FAR_GRP)]
    wait_recv(near_grp, 9)
    p_own = from_groups((0, 1, 3))
    wait_recv(far_grp, 4)
    p_own += from_groups((2,))
    p_out[...] = p_own.astype(BF16)
    for k, step in enumerate(CORE_STEPS):
        send(p_out, p_in.at[k], 5 if k < FAR_CORE else 10, body_peer(step))

    near = near_one(0)
    near_core = p_in.at[pl.ds(FAR_CORE, len(CORE_STEPS) - FAR_CORE)]
    far_core = p_in.at[pl.ds(0, FAR_CORE)]

    def sums(mine, other, low_k, high_k):
        for k in range(low_k, high_k):
            if CORE_STEPS[k][1] == 0:
                mine += p_in[k].astype(F32)
            else:
                other += p_in[k].astype(F32)
        return mine, other

    wait_recv(near_core, 10)
    mine, other = sums(p_own, jnp.zeros_like(p_own), FAR_CORE, len(CORE_STEPS))
    wait_recv(far_core, 5)
    mine, other = sums(mine, other, 0, FAR_CORE)
    z_at = c // 2
    core = c % 2
    i_all[2 * core + z_at] = mine.astype(BF16)
    i_all[2 * core + 1 - z_at] = other.astype(BF16)
    pltpu.make_async_remote_copy(
        src_ref=i_all.at[pl.ds(2 * core, 2)],
        dst_ref=i_all.at[pl.ds(2 * core, 2)],
        send_sem=send_sem.at[7],
        recv_sem=recv_sem.at[7],
        device_id={"grp": g, "body": y * CELL + z_at * 2 + 1 - core},
        device_id_type=pl.DeviceIdType.MESH,
    ).start()

    wait_recv(near_in, 6)
    for k in range(NY - 1):
        near += near_in[k].astype(F32)
    l_exc.wait()
    near_re = v_exc[:, :MODES] + near[:ROWS]
    near_im = v_exc[:, MODES:] + near[ROWS:]

    def from_core(at):
        total = jnp.zeros((2 * ROWS, MODES), F32)
        for z in range(2):
            tile = i_all[2 * at + z]
            rows = pl.ds(pl.multiple_of((2 * z + at) * LANE, LANE), LANE)
            mats = jnp.concatenate([v_down[0, rows, :], v_down[1, rows, :]], axis=0)
            total += dot(paired(tile[:ROWS], tile[ROWS:]), mats)
        return total

    l_down.wait()
    far = from_core(core)
    wait_recv(i_all.at[pl.ds(0, 2)], 7)
    far += from_core(1 - core)
    out[0, :, :MODES] = near_re + far[:ROWS]
    out[0, :, MODES:] = near_im + far[ROWS:]

    wait_send(s_off.at[pl.ds(0, NY - 1)], 0)
    wait_send(scat.at[pl.ds(0, CELL - 1)], 1)
    wait_send(far_body, 2)
    wait_send(near_body, 8)
    wait_send(w_gm.at[:, :, pl.ds(0, CELL - 1)], 3)
    wait_send(far_grp, 4)
    wait_send(near_grp, 9)
    wait_send(far_core, 5)
    wait_send(near_core, 10)
    wait_send(near_in, 6)
    wait_send(i_all.at[pl.ds(0, 2)], 7)


def local(*args):
    anywhere = pl.BlockSpec(memory_space=pl.ANY)
    vmem = pltpu.VMEM
    return pl.pallas_call(
        kernel,
        out_shape=jax.ShapeDtypeStruct((1, ROWS, 2 * MODES), F32),
        in_specs=[anywhere] * 9,
        out_specs=pl.BlockSpec(memory_space=pltpu.VMEM),
        scratch_shapes=[
            vmem((ROWS, 2 * MODES), BF16),
            vmem((ROWS, 2 * MODES), F32),
            vmem((2, MODES, MODES), BF16),
            vmem((225, 2, 512), BF16),
            pltpu.SMEM((NY, 32), jnp.int32),
            pltpu.SMEM((32,), jnp.int32),
            vmem((2, MODES, COEFS), BF16),
            vmem((2, COEFS, MODES), BF16),
            vmem((GRP, 2, CELL, 16, LANE), BF16),
            vmem((CELL, 2 * ROWS, MODES), BF16),
            vmem((NY, 2 * ROWS, MODES), BF16),
            vmem((NY - 1, 2 * ROWS, MODES), BF16),
            vmem((NY, ROWS, LANE), BF16),
            vmem((NY * CELL - 1, ROWS, LANE), BF16),
            vmem((ROWS, LANE), BF16),
            vmem((GRP, ROWS, LANE), BF16),
            vmem((2 * ROWS, LANE), BF16),
            vmem((len(CORE_STEPS), 2 * ROWS, LANE), BF16),
            vmem((CELL, 2 * ROWS, LANE), BF16),
            pltpu.SemaphoreType.DMA((9,)),
            pltpu.SemaphoreType.DMA((11,)),
            pltpu.SemaphoreType.DMA((11,)),
        ],
        compiler_params=pltpu.CompilerParams(
            collective_id=0, has_side_effects=True, vmem_limit_bytes=32 * 1024 * 1024
        ),
        name="scatter_step",
    )(*[pltpu.with_memory_space_constraint(a, pltpu.HBM) for a in args])


def solution(mesh):
    return jax.shard_map(
        local,
        mesh=mesh,
        in_specs=(
            P(("grp", "body"), None, None),
            P(("grp", "body"), None, None),
            P(("grp", "body"), None, None, None),
            P(),
            P(("grp", "body"), None),
            P("grp"),
            P(("grp", "body"), None, None, None),
            P(("grp", "body"), None, None, None),
            P("grp", None, None, "body", None),
        ),
        out_specs=P(("grp", "body"), None, None),
        check_vma=False,
    )
```

```python
import functools

import jax
import jax.numpy as jnp
from jax import lax
from jax.experimental import pallas as pl
from jax.experimental.pallas import tpu as pltpu
from jax.sharding import PartitionSpec as P

BF16 = jnp.bfloat16
F32 = jnp.float32
LANE = 128
ROWS = 16
HALF = 64
GRP = 16
NY = 8
CELL = 4
MODES = 256
COEFS = 512


def dot(a, b):
    return jnp.dot(a, b, preferred_element_type=F32)


def paired(re, im):
    return jnp.concatenate(
        [jnp.concatenate([re, -im], axis=1), jnp.concatenate([im, re], axis=1)], axis=0
    )


BODY_STEPS = [
    (dy, dc)
    for dy in (4, 3, 5, 2, 6, 1, 7, 0)
    for dc in (2, 3, 1, 0)
    if (dy, dc) != (0, 0)
]
FAR_BODY = 12
Y_STEPS = (4, 3, 5, 2, 6, 1, 7)
CELL_STEPS = (2, 3, 1)
CORE_STEPS = [(dy, dc) for dy in (4, 3, 5, 2, 6, 1, 7, 0) for dc in (2, 0) if (dy, dc) != (0, 0)]
FAR_CORE = 6
GRP_STEPS = sorted(
    [(dx, dz) for dx in range(4) for dz in range(4) if (dx, dz) != (0, 0)],
    key=lambda s: -(min(s[0], 4 - s[0]) + 2 * min(s[1], 4 - s[1])),
)
FAR_GRP = 4
EARLY_GRP = 10


def grp_hops(step):
    return min(step[0], 4 - step[0]) + 2 * min(step[1], 4 - step[1])


def body_hops(step):
    return min(step[0], NY - step[0]) + (0, 0.5, 1, 0.5)[step[1]]


def kernel(
    incident,
    exciting,
    t_maps,
    table,
    offsets,
    slots,
    up_maps,
    down_maps,
    group_maps,
    out,
    v_inc,
    v_exc,
    v_t,
    v_table,
    s_off,
    s_slot,
    v_up,
    v_down,
    w_gm,
    scat,
    near_out,
    near_in,
    u_out,
    u_in,
    g_out,
    g_in,
    p_out,
    p_in,
    i_all,
    load_sem,
    send_sem,
    recv_sem,
):
    g = lax.axis_index("grp")
    b = lax.axis_index("body")
    y = b // CELL
    c = b % CELL
    gx = g // 4
    gz = g % 4

    def quarter(member, low_h=0, high_h=GRP):
        columns = pl.ds(pl.multiple_of(member * LANE, LANE), LANE)
        return group_maps.at[0, pl.ds(low_h, high_h - low_h), :, :, columns]

    def body_peer(step):
        dy, dc = step
        return {"grp": g, "body": lax.rem(y + dy, NY) * CELL + lax.rem(c + dc, CELL)}

    def y_peer(d):
        return body_peer((d, 0))

    def cell_peer(d):
        return body_peer((0, d))

    def grp_peer(step):
        dx, dz = step
        return {"grp": lax.rem(gx + dx, 4) * 4 + lax.rem(gz + dz, 4), "body": b}

    barrier = pltpu.get_barrier_semaphore()
    greeted = [(grp_hops(s), grp_peer, s) for s in GRP_STEPS]
    greeted += [(body_hops(s), body_peer, s) for s in BODY_STEPS]
    for _, peer, step in sorted(greeted, key=lambda entry: -entry[0]):
        pl.semaphore_signal(
            barrier, inc=1, device_id=peer(step), device_id_type=pl.DeviceIdType.MESH
        )

    loads = [
        pltpu.make_async_copy(src, dst, load_sem.at[k])
        for k, (src, dst) in enumerate(
            [
                (incident.at[0], v_inc),
                (t_maps.at[0], v_t),
                (up_maps.at[0], v_up),
                (offsets, s_off.at[pl.ds(0, 1)]),
                (slots, s_slot),
                (table, v_table),
                (quarter(c), w_gm.at[:, :, c]),
                (down_maps.at[0], v_down),
                (exciting.at[0], v_exc),
            ]
        )
    ]
    for copy in loads:
        copy.start()
    l_inc, l_t, l_up, l_off, l_slot, l_table, l_gm, l_down, l_exc = loads

    def send(src, dst, phase, peer):
        pltpu.make_async_remote_copy(
            src_ref=src,
            dst_ref=dst,
            send_sem=send_sem.at[phase],
            recv_sem=recv_sem.at[phase],
            device_id=peer,
            device_id_type=pl.DeviceIdType.MESH,
        ).start()

    def wait_recv(ref, phase):
        pltpu.make_async_copy(ref, ref, recv_sem.at[phase]).wait()

    def wait_send(ref, phase):
        pltpu.make_async_copy(ref, ref, send_sem.at[phase]).wait()

    def send_weights(low_h, high_h):
        for d in CELL_STEPS:
            send(
                quarter(lax.rem(c + d, CELL), low_h, high_h),
                w_gm.at[pl.ds(low_h, high_h - low_h), :, c],
                3,
                cell_peer(d),
            )

    l_inc.wait()
    l_t.wait()
    x = v_inc[...]
    scattered = dot(
        paired(x[:, :MODES], x[:, MODES:]), v_t[...].reshape(2 * MODES, MODES)
    ).astype(BF16)
    scat[c] = scattered
    own_pair = paired(scattered[:ROWS], scattered[ROWS:])

    l_up.wait()
    term = dot(own_pair, v_up[...].reshape(2 * MODES, COEFS))
    low = lax.broadcasted_iota(jnp.int32, (ROWS, LANE), 1) < HALF
    for t in range(4):
        re = term[:ROWS, t * LANE : (t + 1) * LANE]
        im = term[ROWS:, t * LANE : (t + 1) * LANE]
        u_out[2 * t] = jnp.where(low, re, pltpu.roll(im, HALF, 1)).astype(BF16)
        u_out[2 * t + 1] = jnp.where(low, pltpu.roll(re, HALF, 1), im).astype(BF16)
    l_off.wait()

    pl.semaphore_wait(barrier, len(BODY_STEPS) + len(GRP_STEPS))
    for k, step in enumerate(BODY_STEPS):
        phase = 2 if k < FAR_BODY else 8
        send(u_out.at[lax.rem(y + step[0], NY)], u_in.at[k], phase, body_peer(step))
    for d in Y_STEPS:
        send(s_off.at[pl.ds(0, 1)], s_off.at[pl.ds(NY - d, 1)], 0, y_peer(d))
    for d in CELL_STEPS:
        send(scat.at[c], scat.at[c], 1, cell_peer(d))
    send_weights(0, EARLY_GRP)

    near_body = u_in.at[pl.ds(FAR_BODY, len(BODY_STEPS) - FAR_BODY)]
    far_body = u_in.at[pl.ds(0, FAR_BODY)]
    e_sum = u_out[y].astype(F32)
    wait_recv(near_body, 8)
    for k in range(FAR_BODY, len(BODY_STEPS)):
        e_sum += u_in[k].astype(F32)
    wait_recv(far_body, 2)
    for k in range(FAR_BODY):
        e_sum += u_in[k].astype(F32)
    g_out[...] = e_sum.astype(BF16)
    for step in GRP_STEPS:
        send(g_out, g_in.at[g], 4 if step[1] == 2 else 9, grp_peer(step))
    g_in[g] = jnp.zeros((ROWS, LANE), BF16)
    send_weights(EARLY_GRP, GRP)

    l_slot.wait()
    l_table.wait()
    wait_recv(scat.at[pl.ds(0, CELL - 1)], 1)
    wait_recv(s_off.at[pl.ds(0, NY - 1)], 0)
    lane = lax.broadcasted_iota(jnp.int32, (LANE, LANE), 1)
    sub = lax.broadcasted_iota(jnp.int32, (LANE, LANE), 0)
    wrapped = lane < sub

    def toeplitz(row):
        turned = [
            pltpu.roll(
                jnp.broadcast_to(row[:, k * LANE : (k + 1) * LANE], (LANE, LANE)),
                0,
                1,
                stride=1,
                stride_axis=0,
            )
            for k in range(4)
        ]
        wide = [
            jnp.where(wrapped, turned[k], turned[k + 1]).astype(BF16) for k in range(3)
        ]
        return jnp.concatenate(
            [
                jnp.concatenate([wide[1], wide[2]], axis=1),
                jnp.concatenate([wide[0], wide[1]], axis=1),
            ],
            axis=0,
        )

    def near_one(d):
        total = jnp.zeros((2 * ROWS, MODES), F32)
        for k in range(CELL):
            seq = v_table[s_off[d, s_slot[y * CELL + k]]].astype(F32)
            keep = jnp.logical_or(d != 0, k != c)
            seq = jnp.where(keep, seq, 0.0)
            mats = jnp.concatenate([toeplitz(seq[0:1]), toeplitz(seq[1:2])], axis=0)
            source = scat[k]
            total += dot(paired(source[:ROWS], source[ROWS:]), mats)
        return total

    def near_chunk(low, high):
        def one(d, carry):
            near_out[d] = near_one(d).astype(BF16)
            send(near_out.at[d], near_in.at[d - 1], 6, y_peer(d))
            return carry

        lax.fori_loop(low, high, one, 0)

    near_chunk(1, NY)

    l_gm.wait()
    wait_recv(w_gm.at[:, :, pl.ds(0, CELL - 1)], 3)

    def from_groups(z_steps):
        tops, bottoms, mats = [], [], []
        for dz in z_steps:
            for x_at in range(4):
                h = x_at * 4 + lax.rem(gz + dz, 4)
                pair = g_in[h].astype(F32)
                tops.append(jnp.where(low, pair, -pair).astype(BF16))
                bottoms.append(pltpu.roll(pair, HALF, 1).astype(BF16))
                mats.append(w_gm[h].reshape(LANE, LANE))
        left = jnp.concatenate(
            [jnp.concatenate(tops, axis=1), jnp.concatenate(bottoms, axis=1)], axis=0
        )
        return dot(left, jnp.concatenate(mats, axis=0))

    near_grp = g_in.at[pl.ds(0, GRP - 1 - FAR_GRP)]
    far_grp = g_in.at[pl.ds(0, FAR_GRP)]
    wait_recv(near_grp, 9)
    p_own = from_groups((0, 1, 3))
    wait_recv(far_grp, 4)
    p_own += from_groups((2,))
    p_out[...] = p_own.astype(BF16)
    for k, step in enumerate(CORE_STEPS):
        send(p_out, p_in.at[k], 5 if k < FAR_CORE else 10, body_peer(step))

    near = near_one(0)
    near_core = p_in.at[pl.ds(FAR_CORE, len(CORE_STEPS) - FAR_CORE)]
    far_core = p_in.at[pl.ds(0, FAR_CORE)]

    def sums(mine, other, low_k, high_k):
        for k in range(low_k, high_k):
            if CORE_STEPS[k][1] == 0:
                mine += p_in[k].astype(F32)
            else:
                other += p_in[k].astype(F32)
        return mine, other

    wait_recv(near_core, 10)
    mine, other = sums(p_own, jnp.zeros_like(p_own), FAR_CORE, len(CORE_STEPS))
    wait_recv(far_core, 5)
    mine, other = sums(mine, other, 0, FAR_CORE)
    z_at = c // 2
    core = c % 2
    i_all[2 * core + z_at] = mine.astype(BF16)
    i_all[2 * core + 1 - z_at] = other.astype(BF16)
    pltpu.make_async_remote_copy(
        src_ref=i_all.at[pl.ds(2 * core, 2)],
        dst_ref=i_all.at[pl.ds(2 * core, 2)],
        send_sem=send_sem.at[7],
        recv_sem=recv_sem.at[7],
        device_id={"grp": g, "body": y * CELL + z_at * 2 + 1 - core},
        device_id_type=pl.DeviceIdType.MESH,
    ).start()

    wait_recv(near_in, 6)
    for k in range(NY - 1):
        near += near_in[k].astype(F32)
    l_exc.wait()
    near_re = v_exc[:, :MODES] + near[:ROWS]
    near_im = v_exc[:, MODES:] + near[ROWS:]

    def from_core(at):
        total = jnp.zeros((2 * ROWS, MODES), F32)
        for z in range(2):
            tile = i_all[2 * at + z]
            rows = pl.ds(pl.multiple_of((2 * z + at) * LANE, LANE), LANE)
            mats = jnp.concatenate([v_down[0, rows, :], v_down[1, rows, :]], axis=0)
            total += dot(paired(tile[:ROWS], tile[ROWS:]), mats)
        return total

    l_down.wait()
    far = from_core(core)
    wait_recv(i_all.at[pl.ds(0, 2)], 7)
    far += from_core(1 - core)
    out[0, :, :MODES] = near_re + far[:ROWS]
    out[0, :, MODES:] = near_im + far[ROWS:]

    wait_send(s_off.at[pl.ds(0, NY - 1)], 0)
    wait_send(scat.at[pl.ds(0, CELL - 1)], 1)
    wait_send(far_body, 2)
    wait_send(near_body, 8)
    wait_send(w_gm.at[:, :, pl.ds(0, CELL - 1)], 3)
    wait_send(far_grp, 4)
    wait_send(near_grp, 9)
    wait_send(far_core, 5)
    wait_send(near_core, 10)
    wait_send(near_in, 6)
    wait_send(i_all.at[pl.ds(0, 2)], 7)


def local(*args):
    anywhere = pl.BlockSpec(memory_space=pl.ANY)
    vmem = pltpu.VMEM
    return pl.pallas_call(
        kernel,
        out_shape=jax.ShapeDtypeStruct((1, ROWS, 2 * MODES), F32),
        in_specs=[anywhere] * 9,
        out_specs=pl.BlockSpec(memory_space=pltpu.VMEM),
        scratch_shapes=[
            vmem((ROWS, 2 * MODES), BF16),
            vmem((ROWS, 2 * MODES), F32),
            vmem((2, MODES, MODES), BF16),
            vmem((225, 2, 512), BF16),
            pltpu.SMEM((NY, 32), jnp.int32),
            pltpu.SMEM((32,), jnp.int32),
            vmem((2, MODES, COEFS), BF16),
            vmem((2, COEFS, MODES), BF16),
            vmem((GRP, 2, CELL, 16, LANE), BF16),
            vmem((CELL, 2 * ROWS, MODES), BF16),
            vmem((NY, 2 * ROWS, MODES), BF16),
            vmem((NY - 1, 2 * ROWS, MODES), BF16),
            vmem((NY, ROWS, LANE), BF16),
            vmem((NY * CELL - 1, ROWS, LANE), BF16),
            vmem((ROWS, LANE), BF16),
            vmem((GRP, ROWS, LANE), BF16),
            vmem((2 * ROWS, LANE), BF16),
            vmem((len(CORE_STEPS), 2 * ROWS, LANE), BF16),
            vmem((CELL, 2 * ROWS, LANE), BF16),
            pltpu.SemaphoreType.DMA((9,)),
            pltpu.SemaphoreType.DMA((11,)),
            pltpu.SemaphoreType.DMA((11,)),
        ],
        compiler_params=pltpu.CompilerParams(
            collective_id=0, has_side_effects=True, vmem_limit_bytes=32 * 1024 * 1024
        ),
        name="scatter_step",
    )(*[pltpu.with_memory_space_constraint(a, pltpu.HBM) for a in args])


def solution(mesh):
    return jax.shard_map(
        local,
        mesh=mesh,
        in_specs=(
            P(("grp", "body"), None, None),
            P(("grp", "body"), None, None),
            P(("grp", "body"), None, None, None),
            P(),
            P(("grp", "body"), None),
            P("grp"),
            P(("grp", "body"), None, None, None),
            P(("grp", "body"), None, None, None),
            P("grp", None, None, "body", None),
        ),
        out_specs=P(("grp", "body"), None, None),
        check_vma=False,
    )
```

```python
import functools

import jax
import jax.numpy as jnp
from jax import lax
from jax.experimental import pallas as pl
from jax.experimental.pallas import tpu as pltpu
from jax.sharding import PartitionSpec as P

BF16 = jnp.bfloat16
F32 = jnp.float32
LANE = 128
ROWS = 16
HALF = 64
GRP = 16
NY = 8
CELL = 4
MODES = 256
COEFS = 512


def dot(a, b):
    return jnp.dot(a, b, preferred_element_type=F32)


def paired(re, im):
    return jnp.concatenate(
        [jnp.concatenate([re, -im], axis=1), jnp.concatenate([im, re], axis=1)], axis=0
    )


Y_STEPS = [
    (dy, dc)
    for dy in (4, 3, 5, 2, 6, 1, 7, 0)
    for dc in (2, 3, 1, 0)
    if (dy, dc) != (0, 0)
]
FAR_BODY = 12
Y_STEPS = (4, 3, 5, 2, 6, 1, 7)
CELL_STEPS = (2, 3, 1)
CORE_STEPS = [(dy, dc) for dy in (4, 3, 5, 2, 6, 1, 7, 0) for dc in (2, 0) if (dy, dc) != (0, 0)]
FAR_CORE = 6
BODY_STEPS = [*CORE_STEPS, (0, 1), (0, 3)]
GRP_STEPS = sorted(
    [(dx, dz) for dx in range(4) for dz in range(4) if (dx, dz) != (0, 0)],
    key=lambda s: -(min(s[0], 4 - s[0]) + 2 * min(s[1], 4 - s[1])),
)
FAR_GRP = 4
EARLY_GRP = 10


def grp_hops(step):
    return min(step[0], 4 - step[0]) + 2 * min(step[1], 4 - step[1])


def body_hops(step):
    return min(step[0], NY - step[0]) + (0, 0.5, 1, 0.5)[step[1]]


def kernel(
    incident,
    exciting,
    t_maps,
    table,
    offsets,
    slots,
    up_maps,
    down_maps,
    group_maps,
    out,
    v_inc,
    v_exc,
    v_t,
    v_table,
    s_off,
    s_slot,
    v_up,
    v_down,
    w_gm,
    scat,
    near_out,
    near_in,
    u_out,
    u_in,
    e_out,
    e_in,
    g_out,
    g_in,
    p_out,
    p_in,
    i_all,
    load_sem,
    send_sem,
    recv_sem,
):
    g = lax.axis_index("grp")
    b = lax.axis_index("body")
    y = b // CELL
    c = b % CELL
    gx = g // 4
    gz = g % 4

    def quarter(member, low_h=0, high_h=GRP):
        columns = pl.ds(pl.multiple_of(member * LANE, LANE), LANE)
        return group_maps.at[0, pl.ds(low_h, high_h - low_h), :, :, columns]

    def body_peer(step):
        dy, dc = step
        return {"grp": g, "body": lax.rem(y + dy, NY) * CELL + lax.rem(c + dc, CELL)}

    def y_peer(d):
        return body_peer((d, 0))

    def cell_peer(d):
        return body_peer((0, d))

    def grp_peer(step):
        dx, dz = step
        return {"grp": lax.rem(gx + dx, 4) * 4 + lax.rem(gz + dz, 4), "body": b}

    barrier = pltpu.get_barrier_semaphore()
    greeted = [(grp_hops(s), grp_peer, s) for s in GRP_STEPS]
    greeted += [(body_hops(s), body_peer, s) for s in BODY_STEPS]
    for _, peer, step in sorted(greeted, key=lambda entry: -entry[0]):
        pl.semaphore_signal(
            barrier, inc=1, device_id=peer(step), device_id_type=pl.DeviceIdType.MESH
        )

    loads = [
        pltpu.make_async_copy(src, dst, load_sem.at[k])
        for k, (src, dst) in enumerate(
            [
                (incident.at[0], v_inc),
                (t_maps.at[0], v_t),
                (up_maps.at[0], v_up),
                (offsets, s_off.at[pl.ds(0, 1)]),
                (slots, s_slot),
                (table, v_table),
                (quarter(c), w_gm.at[:, :, c]),
                (down_maps.at[0], v_down),
                (exciting.at[0], v_exc),
            ]
        )
    ]
    for copy in loads:
        copy.start()
    l_inc, l_t, l_up, l_off, l_slot, l_table, l_gm, l_down, l_exc = loads

    def send(src, dst, phase, peer):
        pltpu.make_async_remote_copy(
            src_ref=src,
            dst_ref=dst,
            send_sem=send_sem.at[phase],
            recv_sem=recv_sem.at[phase],
            device_id=peer,
            device_id_type=pl.DeviceIdType.MESH,
        ).start()

    def wait_recv(ref, phase):
        pltpu.make_async_copy(ref, ref, recv_sem.at[phase]).wait()

    def wait_send(ref, phase):
        pltpu.make_async_copy(ref, ref, send_sem.at[phase]).wait()

    def send_weights(low_h, high_h):
        for d in CELL_STEPS:
            send(
                quarter(lax.rem(c + d, CELL), low_h, high_h),
                w_gm.at[pl.ds(low_h, high_h - low_h), :, c],
                3,
                cell_peer(d),
            )

    l_inc.wait()
    l_t.wait()
    x = v_inc[...]
    scattered = dot(
        paired(x[:, :MODES], x[:, MODES:]), v_t[...].reshape(2 * MODES, MODES)
    ).astype(BF16)
    scat[c] = scattered
    own_pair = paired(scattered[:ROWS], scattered[ROWS:])

    l_up.wait()
    term = dot(own_pair, v_up[...].reshape(2 * MODES, COEFS))
    low = lax.broadcasted_iota(jnp.int32, (ROWS, LANE), 1) < HALF
    for t in range(4):
        re = term[:ROWS, t * LANE : (t + 1) * LANE]
        im = term[ROWS:, t * LANE : (t + 1) * LANE]
        u_out[2 * t] = jnp.where(low, re, pltpu.roll(im, HALF, 1)).astype(BF16)
        u_out[2 * t + 1] = jnp.where(low, pltpu.roll(re, HALF, 1), im).astype(BF16)
    l_off.wait()

    pl.semaphore_wait(barrier, len(BODY_STEPS) + len(GRP_STEPS))
    for k, step in enumerate(CORE_STEPS):
        phase = 2 if k < FAR_CORE else 8
        send(u_out.at[lax.rem(y + step[0], NY)], u_in.at[k], phase, body_peer(step))
    for d in Y_STEPS:
        send(s_off.at[pl.ds(0, 1)], s_off.at[pl.ds(NY - d, 1)], 0, y_peer(d))
    for d in CELL_STEPS:
        send(scat.at[c], scat.at[c], 1, cell_peer(d))
    send_weights(0, EARLY_GRP)

    near_body = u_in.at[pl.ds(FAR_CORE, len(CORE_STEPS) - FAR_CORE)]
    far_body = u_in.at[pl.ds(0, FAR_CORE)]
    e_sum = u_out[y].astype(F32)
    wait_recv(near_body, 8)
    for k in range(FAR_CORE, len(CORE_STEPS)):
        e_sum += u_in[k].astype(F32)
    wait_recv(far_body, 2)
    for k in range(FAR_CORE):
        e_sum += u_in[k].astype(F32)
    e_out[...] = e_sum
    z_at = c // 2
    core = c % 2
    other_core = {"grp": g, "body": y * CELL + z_at * 2 + 1 - core}
    send(e_out, e_in, 11, other_core)
    wait_recv(e_in, 11)
    e_sum += e_in[...]
    g_out[...] = e_sum.astype(BF16)
    for step in GRP_STEPS:
        send(g_out, g_in.at[g], 4 if step[1] == 2 else 9, grp_peer(step))
    g_in[g] = jnp.zeros((ROWS, LANE), BF16)
    send_weights(EARLY_GRP, GRP)

    l_slot.wait()
    l_table.wait()
    wait_recv(scat.at[pl.ds(0, CELL - 1)], 1)
    wait_recv(s_off.at[pl.ds(0, NY - 1)], 0)
    lane = lax.broadcasted_iota(jnp.int32, (LANE, LANE), 1)
    sub = lax.broadcasted_iota(jnp.int32, (LANE, LANE), 0)
    wrapped = lane < sub

    def toeplitz(row):
        turned = [
            pltpu.roll(
                jnp.broadcast_to(row[:, k * LANE : (k + 1) * LANE], (LANE, LANE)),
                0,
                1,
                stride=1,
                stride_axis=0,
            )
            for k in range(4)
        ]
        wide = [
            jnp.where(wrapped, turned[k], turned[k + 1]).astype(BF16) for k in range(3)
        ]
        return jnp.concatenate(
            [
                jnp.concatenate([wide[1], wide[2]], axis=1),
                jnp.concatenate([wide[0], wide[1]], axis=1),
            ],
            axis=0,
        )

    def near_one(d):
        total = jnp.zeros((2 * ROWS, MODES), F32)
        for k in range(CELL):
            seq = v_table[s_off[d, s_slot[y * CELL + k]]].astype(F32)
            keep = jnp.logical_or(d != 0, k != c)
            seq = jnp.where(keep, seq, 0.0)
            mats = jnp.concatenate([toeplitz(seq[0:1]), toeplitz(seq[1:2])], axis=0)
            source = scat[k]
            total += dot(paired(source[:ROWS], source[ROWS:]), mats)
        return total

    def near_chunk(low, high):
        def one(d, carry):
            near_out[d] = near_one(d).astype(BF16)
            send(near_out.at[d], near_in.at[d - 1], 6, y_peer(d))
            return carry

        lax.fori_loop(low, high, one, 0)

    near_chunk(1, NY)

    l_gm.wait()
    wait_recv(w_gm.at[:, :, pl.ds(0, CELL - 1)], 3)

    def from_groups(z_steps):
        tops, bottoms, mats = [], [], []
        for dz in z_steps:
            for x_at in range(4):
                h = x_at * 4 + lax.rem(gz + dz, 4)
                pair = g_in[h].astype(F32)
                tops.append(jnp.where(low, pair, -pair).astype(BF16))
                bottoms.append(pltpu.roll(pair, HALF, 1).astype(BF16))
                mats.append(w_gm[h].reshape(LANE, LANE))
        left = jnp.concatenate(
            [jnp.concatenate(tops, axis=1), jnp.concatenate(bottoms, axis=1)], axis=0
        )
        return dot(left, jnp.concatenate(mats, axis=0))

    near_grp = g_in.at[pl.ds(0, GRP - 1 - FAR_GRP)]
    far_grp = g_in.at[pl.ds(0, FAR_GRP)]
    wait_recv(near_grp, 9)
    p_own = from_groups((0, 1, 3))
    wait_recv(far_grp, 4)
    p_own += from_groups((2,))
    p_out[...] = p_own.astype(BF16)
    for k, step in enumerate(CORE_STEPS):
        send(p_out, p_in.at[k], 5 if k < FAR_CORE else 10, body_peer(step))

    near = near_one(0)
    near_core = p_in.at[pl.ds(FAR_CORE, len(CORE_STEPS) - FAR_CORE)]
    far_core = p_in.at[pl.ds(0, FAR_CORE)]

    def sums(mine, other, low_k, high_k):
        for k in range(low_k, high_k):
            if CORE_STEPS[k][1] == 0:
                mine += p_in[k].astype(F32)
            else:
                other += p_in[k].astype(F32)
        return mine, other

    wait_recv(near_core, 10)
    mine, other = sums(p_own, jnp.zeros_like(p_own), FAR_CORE, len(CORE_STEPS))
    wait_recv(far_core, 5)
    mine, other = sums(mine, other, 0, FAR_CORE)
    i_all[2 * core + z_at] = mine.astype(BF16)
    i_all[2 * core + 1 - z_at] = other.astype(BF16)
    pair_of_core = i_all.at[pl.ds(2 * core, 2)]
    send(pair_of_core, pair_of_core, 7, other_core)

    wait_recv(near_in, 6)
    for k in range(NY - 1):
        near += near_in[k].astype(F32)
    l_exc.wait()
    near_re = v_exc[:, :MODES] + near[:ROWS]
    near_im = v_exc[:, MODES:] + near[ROWS:]

    def from_core(at):
        total = jnp.zeros((2 * ROWS, MODES), F32)
        for z in range(2):
            tile = i_all[2 * at + z]
            rows = pl.ds(pl.multiple_of((2 * z + at) * LANE, LANE), LANE)
            mats = jnp.concatenate([v_down[0, rows, :], v_down[1, rows, :]], axis=0)
            total += dot(paired(tile[:ROWS], tile[ROWS:]), mats)
        return total

    l_down.wait()
    far = from_core(core)
    wait_recv(i_all.at[pl.ds(0, 2)], 7)
    far += from_core(1 - core)
    out[0, :, :MODES] = near_re + far[:ROWS]
    out[0, :, MODES:] = near_im + far[ROWS:]

    wait_send(s_off.at[pl.ds(0, NY - 1)], 0)
    wait_send(scat.at[pl.ds(0, CELL - 1)], 1)
    wait_send(far_body, 2)
    wait_send(near_body, 8)
    wait_send(e_in, 11)
    wait_send(w_gm.at[:, :, pl.ds(0, CELL - 1)], 3)
    wait_send(far_grp, 4)
    wait_send(near_grp, 9)
    wait_send(far_core, 5)
    wait_send(near_core, 10)
    wait_send(near_in, 6)
    wait_send(i_all.at[pl.ds(0, 2)], 7)


def local(*args):
    anywhere = pl.BlockSpec(memory_space=pl.ANY)
    vmem = pltpu.VMEM
    return pl.pallas_call(
        kernel,
        out_shape=jax.ShapeDtypeStruct((1, ROWS, 2 * MODES), F32),
        in_specs=[anywhere] * 9,
        out_specs=pl.BlockSpec(memory_space=pltpu.VMEM),
        scratch_shapes=[
            vmem((ROWS, 2 * MODES), BF16),
            vmem((ROWS, 2 * MODES), F32),
            vmem((2, MODES, MODES), BF16),
            vmem((225, 2, 512), BF16),
            pltpu.SMEM((NY, 32), jnp.int32),
            pltpu.SMEM((32,), jnp.int32),
            vmem((2, MODES, COEFS), BF16),
            vmem((2, COEFS, MODES), BF16),
            vmem((GRP, 2, CELL, 16, LANE), BF16),
            vmem((CELL, 2 * ROWS, MODES), BF16),
            vmem((NY, 2 * ROWS, MODES), BF16),
            vmem((NY - 1, 2 * ROWS, MODES), BF16),
            vmem((NY, ROWS, LANE), BF16),
            vmem((len(CORE_STEPS), ROWS, LANE), BF16),
            vmem((ROWS, LANE), F32),
            vmem((ROWS, LANE), F32),
            vmem((ROWS, LANE), BF16),
            vmem((GRP, ROWS, LANE), BF16),
            vmem((2 * ROWS, LANE), BF16),
            vmem((len(CORE_STEPS), 2 * ROWS, LANE), BF16),
            vmem((CELL, 2 * ROWS, LANE), BF16),
            pltpu.SemaphoreType.DMA((9,)),
            pltpu.SemaphoreType.DMA((12,)),
            pltpu.SemaphoreType.DMA((12,)),
        ],
        compiler_params=pltpu.CompilerParams(
            collective_id=0, has_side_effects=True, vmem_limit_bytes=32 * 1024 * 1024
        ),
        name="scatter_step",
    )(*[pltpu.with_memory_space_constraint(a, pltpu.HBM) for a in args])


def solution(mesh):
    return jax.shard_map(
        local,
        mesh=mesh,
        in_specs=(
            P(("grp", "body"), None, None),
            P(("grp", "body"), None, None),
            P(("grp", "body"), None, None, None),
            P(),
            P(("grp", "body"), None),
            P("grp"),
            P(("grp", "body"), None, None, None),
            P(("grp", "body"), None, None, None),
            P("grp", None, None, "body", None),
        ),
        out_specs=P(("grp", "body"), None, None),
        check_vma=False,
    )
```

```python
import functools

import jax
import jax.numpy as jnp
from jax import lax
from jax.experimental import pallas as pl
from jax.experimental.pallas import tpu as pltpu
from jax.sharding import PartitionSpec as P

BF16 = jnp.bfloat16
F32 = jnp.float32
LANE = 128
ROWS = 16
HALF = 64
GRP = 16
NY = 8
CELL = 4
MODES = 256
COEFS = 512


def dot(a, b):
    return jnp.dot(a, b, preferred_element_type=F32)


def paired(re, im):
    return jnp.concatenate(
        [jnp.concatenate([re, -im], axis=1), jnp.concatenate([im, re], axis=1)], axis=0
    )


Y_STEPS = [
    (dy, dc)
    for dy in (4, 3, 5, 2, 6, 1, 7, 0)
    for dc in (2, 3, 1, 0)
    if (dy, dc) != (0, 0)
]
FAR_BODY = 12
Y_STEPS = (4, 3, 5, 2, 6, 1, 7)
CELL_STEPS = (2, 3, 1)
CORE_STEPS = [(dy, dc) for dy in (4, 3, 5, 2, 6, 1, 7, 0) for dc in (2, 0) if (dy, dc) != (0, 0)]
FAR_CORE = 6
BODY_STEPS = [*CORE_STEPS, (0, 1), (0, 3)]
GRP_STEPS = sorted(
    [(dx, dz) for dx in range(4) for dz in range(4) if (dx, dz) != (0, 0)],
    key=lambda s: -(min(s[0], 4 - s[0]) + 2 * min(s[1], 4 - s[1])),
)
FAR_GRP = 4
EARLY_GRP = 10


def grp_hops(step):
    return min(step[0], 4 - step[0]) + 2 * min(step[1], 4 - step[1])


def body_hops(step):
    return min(step[0], NY - step[0]) + (0, 0.5, 1, 0.5)[step[1]]


def kernel(
    incident,
    exciting,
    t_maps,
    table,
    offsets,
    slots,
    up_maps,
    down_maps,
    group_maps,
    out,
    v_inc,
    v_exc,
    v_t,
    v_table,
    s_off,
    s_slot,
    v_up,
    v_down,
    w_gm,
    scat,
    near_out,
    near_in,
    u_out,
    u_in,
    e_out,
    e_in,
    g_out,
    g_in,
    p_out,
    p_in,
    i_all,
    load_sem,
    send_sem,
    recv_sem,
):
    g = lax.axis_index("grp")
    b = lax.axis_index("body")
    y = b // CELL
    c = b % CELL
    gx = g // 4
    gz = g % 4

    def quarter(member, low_h=0, high_h=GRP):
        columns = pl.ds(pl.multiple_of(member * LANE, LANE), LANE)
        return group_maps.at[0, pl.ds(low_h, high_h - low_h), :, :, columns]

    def body_peer(step):
        dy, dc = step
        return {"grp": g, "body": lax.rem(y + dy, NY) * CELL + lax.rem(c + dc, CELL)}

    def y_peer(d):
        return body_peer((d, 0))

    def cell_peer(d):
        return body_peer((0, d))

    def grp_peer(step):
        dx, dz = step
        return {"grp": lax.rem(gx + dx, 4) * 4 + lax.rem(gz + dz, 4), "body": b}

    loads = [
        pltpu.make_async_copy(src, dst, load_sem.at[k])
        for k, (src, dst) in enumerate(
            [
                (incident.at[0], v_inc),
                (t_maps.at[0], v_t),
                (up_maps.at[0], v_up),
                (offsets, s_off.at[pl.ds(0, 1)]),
                (slots, s_slot),
                (table, v_table),
                (quarter(c), w_gm.at[:, :, c]),
                (down_maps.at[0], v_down),
                (exciting.at[0], v_exc),
            ]
        )
    ]
    l_inc, l_t, l_up, l_off, l_slot, l_table, l_gm, l_down, l_exc = loads
    for copy in loads[:3]:
        copy.start()
    barrier = pltpu.get_barrier_semaphore()
    greeted = [(grp_hops(s), grp_peer, s) for s in GRP_STEPS]
    greeted += [(body_hops(s), body_peer, s) for s in BODY_STEPS]
    for _, peer, step in sorted(greeted, key=lambda entry: -entry[0]):
        pl.semaphore_signal(
            barrier, inc=1, device_id=peer(step), device_id_type=pl.DeviceIdType.MESH
        )

    for copy in loads[3:]:
        copy.start()

    def send(src, dst, phase, peer):
        pltpu.make_async_remote_copy(
            src_ref=src,
            dst_ref=dst,
            send_sem=send_sem.at[phase],
            recv_sem=recv_sem.at[phase],
            device_id=peer,
            device_id_type=pl.DeviceIdType.MESH,
        ).start()

    def wait_recv(ref, phase):
        pltpu.make_async_copy(ref, ref, recv_sem.at[phase]).wait()

    def wait_send(ref, phase):
        pltpu.make_async_copy(ref, ref, send_sem.at[phase]).wait()

    def send_weights(low_h, high_h):
        for d in CELL_STEPS:
            send(
                quarter(lax.rem(c + d, CELL), low_h, high_h),
                w_gm.at[pl.ds(low_h, high_h - low_h), :, c],
                3,
                cell_peer(d),
            )

    l_inc.wait()
    l_t.wait()
    x = v_inc[...]
    scattered = dot(
        paired(x[:, :MODES], x[:, MODES:]), v_t[...].reshape(2 * MODES, MODES)
    ).astype(BF16)
    scat[c] = scattered
    own_pair = paired(scattered[:ROWS], scattered[ROWS:])

    l_up.wait()
    term = dot(own_pair, v_up[...].reshape(2 * MODES, COEFS))
    low = lax.broadcasted_iota(jnp.int32, (ROWS, LANE), 1) < HALF
    for t in range(4):
        re = term[:ROWS, t * LANE : (t + 1) * LANE]
        im = term[ROWS:, t * LANE : (t + 1) * LANE]
        u_out[2 * t] = jnp.where(low, re, pltpu.roll(im, HALF, 1)).astype(BF16)
        u_out[2 * t + 1] = jnp.where(low, pltpu.roll(re, HALF, 1), im).astype(BF16)
    l_off.wait()

    pl.semaphore_wait(barrier, len(BODY_STEPS) + len(GRP_STEPS))
    for k, step in enumerate(CORE_STEPS):
        phase = 2 if k < FAR_CORE else 8
        send(u_out.at[lax.rem(y + step[0], NY)], u_in.at[k], phase, body_peer(step))
    for d in Y_STEPS:
        send(s_off.at[pl.ds(0, 1)], s_off.at[pl.ds(NY - d, 1)], 0, y_peer(d))
    for d in CELL_STEPS:
        send(scat.at[c], scat.at[c], 1, cell_peer(d))
    send_weights(0, EARLY_GRP)

    near_body = u_in.at[pl.ds(FAR_CORE, len(CORE_STEPS) - FAR_CORE)]
    far_body = u_in.at[pl.ds(0, FAR_CORE)]
    e_sum = u_out[y].astype(F32)
    wait_recv(near_body, 8)
    for k in range(FAR_CORE, len(CORE_STEPS)):
        e_sum += u_in[k].astype(F32)
    wait_recv(far_body, 2)
    for k in range(FAR_CORE):
        e_sum += u_in[k].astype(F32)
    e_out[...] = e_sum
    z_at = c // 2
    core = c % 2
    other_core = {"grp": g, "body": y * CELL + z_at * 2 + 1 - core}
    send(e_out, e_in, 11, other_core)
    wait_recv(e_in, 11)
    e_sum += e_in[...]
    g_out[...] = e_sum.astype(BF16)
    for step in GRP_STEPS:
        send(g_out, g_in.at[g], 4 if step[1] == 2 else 9, grp_peer(step))
    g_in[g] = jnp.zeros((ROWS, LANE), BF16)
    send_weights(EARLY_GRP, GRP)

    l_slot.wait()
    l_table.wait()
    wait_recv(scat.at[pl.ds(0, CELL - 1)], 1)
    wait_recv(s_off.at[pl.ds(0, NY - 1)], 0)
    lane = lax.broadcasted_iota(jnp.int32, (LANE, LANE), 1)
    sub = lax.broadcasted_iota(jnp.int32, (LANE, LANE), 0)
    wrapped = lane < sub

    def toeplitz(row):
        turned = [
            pltpu.roll(
                jnp.broadcast_to(row[:, k * LANE : (k + 1) * LANE], (LANE, LANE)),
                0,
                1,
                stride=1,
                stride_axis=0,
            )
            for k in range(4)
        ]
        wide = [
            jnp.where(wrapped, turned[k], turned[k + 1]).astype(BF16) for k in range(3)
        ]
        return jnp.concatenate(
            [
                jnp.concatenate([wide[1], wide[2]], axis=1),
                jnp.concatenate([wide[0], wide[1]], axis=1),
            ],
            axis=0,
        )

    def near_one(d):
        total = jnp.zeros((2 * ROWS, MODES), F32)
        for k in range(CELL):
            seq = v_table[s_off[d, s_slot[y * CELL + k]]].astype(F32)
            keep = jnp.logical_or(d != 0, k != c)
            seq = jnp.where(keep, seq, 0.0)
            mats = jnp.concatenate([toeplitz(seq[0:1]), toeplitz(seq[1:2])], axis=0)
            source = scat[k]
            total += dot(paired(source[:ROWS], source[ROWS:]), mats)
        return total

    def near_chunk(low, high):
        def one(d, carry):
            near_out[d] = near_one(d).astype(BF16)
            send(near_out.at[d], near_in.at[d - 1], 6, y_peer(d))
            return carry

        lax.fori_loop(low, high, one, 0)

    near_chunk(1, NY)

    l_gm.wait()
    wait_recv(w_gm.at[:, :, pl.ds(0, CELL - 1)], 3)

    def from_groups(z_steps):
        tops, bottoms, mats = [], [], []
        for dz in z_steps:
            for x_at in range(4):
                h = x_at * 4 + lax.rem(gz + dz, 4)
                pair = g_in[h].astype(F32)
                tops.append(jnp.where(low, pair, -pair).astype(BF16))
                bottoms.append(pltpu.roll(pair, HALF, 1).astype(BF16))
                mats.append(w_gm[h].reshape(LANE, LANE))
        left = jnp.concatenate(
            [jnp.concatenate(tops, axis=1), jnp.concatenate(bottoms, axis=1)], axis=0
        )
        return dot(left, jnp.concatenate(mats, axis=0))

    near_grp = g_in.at[pl.ds(0, GRP - 1 - FAR_GRP)]
    far_grp = g_in.at[pl.ds(0, FAR_GRP)]
    wait_recv(near_grp, 9)
    p_own = from_groups((0, 1, 3))
    wait_recv(far_grp, 4)
    p_own += from_groups((2,))
    p_out[...] = p_own.astype(BF16)
    for k, step in enumerate(CORE_STEPS):
        send(p_out, p_in.at[k], 5 if k < FAR_CORE else 10, body_peer(step))

    near = near_one(0)
    near_core = p_in.at[pl.ds(FAR_CORE, len(CORE_STEPS) - FAR_CORE)]
    far_core = p_in.at[pl.ds(0, FAR_CORE)]

    def sums(mine, other, low_k, high_k):
        for k in range(low_k, high_k):
            if CORE_STEPS[k][1] == 0:
                mine += p_in[k].astype(F32)
            else:
                other += p_in[k].astype(F32)
        return mine, other

    wait_recv(near_core, 10)
    mine, other = sums(p_own, jnp.zeros_like(p_own), FAR_CORE, len(CORE_STEPS))
    wait_recv(far_core, 5)
    mine, other = sums(mine, other, 0, FAR_CORE)
    i_all[2 * core + z_at] = mine.astype(BF16)
    i_all[2 * core + 1 - z_at] = other.astype(BF16)
    pair_of_core = i_all.at[pl.ds(2 * core, 2)]
    send(pair_of_core, pair_of_core, 7, other_core)

    wait_recv(near_in, 6)
    for k in range(NY - 1):
        near += near_in[k].astype(F32)
    l_exc.wait()
    near_re = v_exc[:, :MODES] + near[:ROWS]
    near_im = v_exc[:, MODES:] + near[ROWS:]

    def from_core(at):
        total = jnp.zeros((2 * ROWS, MODES), F32)
        for z in range(2):
            tile = i_all[2 * at + z]
            rows = pl.ds(pl.multiple_of((2 * z + at) * LANE, LANE), LANE)
            mats = jnp.concatenate([v_down[0, rows, :], v_down[1, rows, :]], axis=0)
            total += dot(paired(tile[:ROWS], tile[ROWS:]), mats)
        return total

    l_down.wait()
    far = from_core(core)
    wait_recv(i_all.at[pl.ds(0, 2)], 7)
    far += from_core(1 - core)
    out[0, :, :MODES] = near_re + far[:ROWS]
    out[0, :, MODES:] = near_im + far[ROWS:]

    wait_send(s_off.at[pl.ds(0, NY - 1)], 0)
    wait_send(scat.at[pl.ds(0, CELL - 1)], 1)
    wait_send(far_body, 2)
    wait_send(near_body, 8)
    wait_send(e_in, 11)
    wait_send(w_gm.at[:, :, pl.ds(0, CELL - 1)], 3)
    wait_send(far_grp, 4)
    wait_send(near_grp, 9)
    wait_send(far_core, 5)
    wait_send(near_core, 10)
    wait_send(near_in, 6)
    wait_send(i_all.at[pl.ds(0, 2)], 7)


def local(*args):
    anywhere = pl.BlockSpec(memory_space=pl.ANY)
    vmem = pltpu.VMEM
    return pl.pallas_call(
        kernel,
        out_shape=jax.ShapeDtypeStruct((1, ROWS, 2 * MODES), F32),
        in_specs=[anywhere] * 9,
        out_specs=pl.BlockSpec(memory_space=pltpu.VMEM),
        scratch_shapes=[
            vmem((ROWS, 2 * MODES), BF16),
            vmem((ROWS, 2 * MODES), F32),
            vmem((2, MODES, MODES), BF16),
            vmem((225, 2, 512), BF16),
            pltpu.SMEM((NY, 32), jnp.int32),
            pltpu.SMEM((32,), jnp.int32),
            vmem((2, MODES, COEFS), BF16),
            vmem((2, COEFS, MODES), BF16),
            vmem((GRP, 2, CELL, 16, LANE), BF16),
            vmem((CELL, 2 * ROWS, MODES), BF16),
            vmem((NY, 2 * ROWS, MODES), BF16),
            vmem((NY - 1, 2 * ROWS, MODES), BF16),
            vmem((NY, ROWS, LANE), BF16),
            vmem((len(CORE_STEPS), ROWS, LANE), BF16),
            vmem((ROWS, LANE), F32),
            vmem((ROWS, LANE), F32),
            vmem((ROWS, LANE), BF16),
            vmem((GRP, ROWS, LANE), BF16),
            vmem((2 * ROWS, LANE), BF16),
            vmem((len(CORE_STEPS), 2 * ROWS, LANE), BF16),
            vmem((CELL, 2 * ROWS, LANE), BF16),
            pltpu.SemaphoreType.DMA((9,)),
            pltpu.SemaphoreType.DMA((12,)),
            pltpu.SemaphoreType.DMA((12,)),
        ],
        compiler_params=pltpu.CompilerParams(
            collective_id=0, has_side_effects=True, vmem_limit_bytes=32 * 1024 * 1024
        ),
        name="scatter_step",
    )(*[pltpu.with_memory_space_constraint(a, pltpu.HBM) for a in args])


def solution(mesh):
    return jax.shard_map(
        local,
        mesh=mesh,
        in_specs=(
            P(("grp", "body"), None, None),
            P(("grp", "body"), None, None),
            P(("grp", "body"), None, None, None),
            P(),
            P(("grp", "body"), None),
            P("grp"),
            P(("grp", "body"), None, None, None),
            P(("grp", "body"), None, None, None),
            P("grp", None, None, "body", None),
        ),
        out_specs=P(("grp", "body"), None, None),
        check_vma=False,
    )
```
